256 devices in a mesh: expert: 64 (over y, z_hi, x), zero: 4 (over z_lo, core).
Axes of the slice: x: 4, y: 4, z: 8 (z_hi: 4, z_lo: 2; z = z_hi * 2 + z_lo), core: 2. Of those that a mesh axis runs over, the one named last changes fastest.
Arguments:
- tokens: bfloat16 [32768, 3584], P(('expert', 'zero')), may hold values from -6 to 6
- accepted: int32 [32768], P(('expert', 'zero')), may hold values from 0 to 1, as said below
- routes: int32 [32768, 8], P(('expert', 'zero')), may hold values from 0 to 63, as said below
- gates: float32 [32768, 8], P(('expert', 'zero')), may hold values from 0.1 to 1
- partner: int32 [64], replicated, may hold values from 0 to 63, as said below
- w_gate: bfloat16 [64, 3584, 1024], P('expert', None, 'zero'), may hold values from -0.09375 to 0.09375
- w_up: bfloat16 [64, 3584, 1024], P('expert', None, 'zero'), may hold values from -0.09375 to 0.09375
- w_down: bfloat16 [64, 1024, 3584], P('expert', 'zero'), may hold values from -0.1875 to 0.1875
- master_rows: float32 [64, 32, 3584], P('expert', 'zero'), may hold values from -6 to 6
- first_moment: float32 [64, 32, 3584], P('expert', 'zero'), may hold values from -6 to 6
- second_moment: float32 [64, 32, 3584], P('expert', 'zero'), may hold values from 0.1 to 2
Outputs:
- combined: bfloat16 [32768, 3584], P(('expert', 'zero'))
- new_gate: bfloat16 [64, 3584, 1024], P('expert', None, 'zero')
- new_up: bfloat16 [64, 3584, 1024], P('expert', None, 'zero')
- new_down: bfloat16 [64, 1024, 3584], P('expert', 'zero')
- new_master: float32 [64, 32, 3584], P('expert', 'zero')
- new_first: float32 [64, 32, 3584], P('expert', 'zero')
- new_second: float32 [64, 32, 3584], P('expert', 'zero')
The draws below stay inside these ranges and needn't reach their ends.
Inputs may be any that keep to these rules, and one draw needn't show every extreme that they name: `accepted`: exactly 32 rows of each device's 128 rows are 1. `routes`: each row names 8 different experts. Over the accepted rows of one device no expert is named more than 8 times, and some expert exactly 8 times. partner[partner[i]] = i, and partner[i] is i or i plus or minus 64 // 2.
All inputs are finite; a program needn't handle non-finite values.
Results may differ from the reference program's by a relative error of at most 0.0065.
Values may be sent and summed in bfloat16 or wider, within the bound.
A program may use at most 128 MiB of HBM per device.

```python
import math
import jax
import jax.numpy as jnp
from jax import lax

D = 3584
TOPK = 8
TOK_DEV = 128
EXPERTS = 64
FF = 1024
ACC_DEV = 32
CAP = 8
TOKENS = 32768
BUCKET = 32
N_EXPERT = 64
N_ZERO = 4


def route_blocks(key):
    blocks = TOKENS // TOK_DEV
    groups = EXPERTS // TOPK
    others = max(groups - 1, 1)

    def one_block(block_key):
        key_pick, key_class, key_other, key_order = jax.random.split(block_key, 4)
        pick = jax.random.permutation(key_pick, TOK_DEV).astype(jnp.int32)
        placed = jnp.argsort(pick, stable=True).astype(jnp.int32)
        taken = (placed < ACC_DEV).astype(jnp.int32)
        classes = jax.random.permutation(key_class, groups).astype(jnp.int32)
        spread = jnp.where(placed < CAP, 0, 1 + (placed - CAP) % others)
        spread = jnp.minimum(spread, groups - 1).astype(jnp.int32)
        other_class = jax.random.randint(key_other, (TOK_DEV,), 0, groups).astype(jnp.int32)
        chosen = jnp.where(placed < ACC_DEV, classes[spread], other_class)
        order = jax.random.permutation(key_order, EXPERTS).astype(jnp.int32)
        slots = groups * jnp.arange(TOPK, dtype=jnp.int32)[None, :] + chosen[:, None]
        return (taken, order[slots])
    keys = jax.random.split(key, blocks)
    taken, named = jax.vmap(one_block)(keys)
    return (taken.reshape(TOKENS), named.reshape(TOKENS, TOPK))


def draw_accepted(key, part):
    taken, named = route_blocks(key)
    return taken


def draw_routes(key, part):
    taken, named = route_blocks(key)
    return named


def draw_partner(key, part):
    key = jax.random.fold_in(key, 7)
    half = EXPERTS // 2
    flips = jax.random.randint(key, (half,), 0, 2).astype(jnp.int32)
    lower = jnp.arange(half, dtype=jnp.int32)
    return jnp.concatenate([lower + flips * half, lower + half - flips * half]).astype(jnp.int32)


def levels(key, dims, cuts, smallest, high):
    def one(axis_at, parts):
        draws = jax.random.uniform(jax.random.fold_in(jax.random.fold_in(key, 6), axis_at), (parts,), jnp.float32, smallest / len(cuts), high / len(cuts))
        return jnp.repeat(jnp.exp(draws), dims[axis_at] // parts).reshape((-1,) + (1,) * (len(dims) - axis_at - 1))

    gain = one(*cuts[0])
    for cut in cuts[1:]:
        gain = gain * one(*cut)
    return gain


def normal_values(stream_key, dims, width, bound, cuts=(), kind=jnp.bfloat16):
    values = jax.random.normal(stream_key, dims, jnp.float32) * width
    if len(cuts) > 0:
        values = levels(stream_key, dims, cuts, -0.22, 0.18) * values
    return jnp.clip(values, min=-bound, max=bound).astype(kind)


def setup_inputs(seed: int = 0) -> dict:
    key_list = jax.random.split(jax.random.key(seed), 12)
    return {
        "tokens": normal_values(key_list[0], (TOKENS, D), 1.0, 6.0, ((0, 256),)),
        "accepted": draw_accepted(jax.random.fold_in(key_list[11], 71), 0),
        "routes": draw_routes(jax.random.fold_in(key_list[11], 71), 0),
        "gates": jnp.clip(jnp.exp(math.log(1.0) - 2.3025851 * jax.random.uniform(key_list[3], (TOKENS, TOPK), jnp.float32) ** levels(key_list[3], (TOKENS, TOPK), ((0, 256),), -0.2, 0.2)), 0.1, 1.0),
        "partner": draw_partner(jax.random.fold_in(key_list[11], 71), 0),
        "w_gate": normal_values(key_list[5], (EXPERTS, D, FF), D ** -0.5, 0.09375, ((0, 64), (2, 4))),
        "w_up": normal_values(key_list[6], (EXPERTS, D, FF), D ** -0.5, 0.09375, ((0, 64), (2, 4))),
        "w_down": normal_values(key_list[7], (EXPERTS, FF, D), FF ** -0.5, 0.1875, ((0, 64), (1, 4))),
        "master_rows": normal_values(key_list[8], (EXPERTS, BUCKET, D), 1.0, 6.0, ((0, 64), (1, 4)), jnp.float32),
        "first_moment": normal_values(key_list[9], (EXPERTS, BUCKET, D), 1.0, 6.0, ((0, 64), (1, 4)), jnp.float32),
        "second_moment": jnp.clip(jnp.exp(math.log(2.0) - 2.9957323 * jax.random.uniform(key_list[10], (EXPERTS, BUCKET, D), jnp.float32) ** levels(key_list[10], (EXPERTS, BUCKET, D), ((0, 64), (1, 4)), -0.2, 0.2)), 0.1, 2.0),
    }


def reference(tokens, accepted, routes, gates, partner, w_gate, w_up, w_down, master_rows, first_moment, second_moment):
    pairs = TOKENS * TOPK
    flat_route = routes.reshape(pairs)
    flat_token = (jnp.arange(pairs, dtype=jnp.int32) // TOPK).astype(jnp.int32)
    flat_gate = gates.reshape(pairs)
    flat_keep = accepted[flat_token]
    most = CAP * N_EXPERT * N_ZERO

    def add_expert(index, total):
        match = (flat_route == index) & (flat_keep == 1)
        order = jnp.argsort(jnp.where(match, 0, 1).astype(jnp.int32), stable=True)[:most].astype(jnp.int32)
        valid = match[order]
        owner = flat_token[order]
        rows = tokens[owner]
        gate = jnp.dot(rows, w_gate[index], preferred_element_type=jnp.float32)
        up = jnp.dot(rows, w_up[index], preferred_element_type=jnp.float32)
        hidden = (jax.nn.silu(gate) * up).astype(jnp.bfloat16)
        expert_out = jnp.dot(hidden, w_down[index], preferred_element_type=jnp.float32).astype(jnp.bfloat16)
        expert_out = lax.optimization_barrier(expert_out).astype(jnp.float32)
        weight = jnp.where(valid, flat_gate[order], jnp.float32(0.0))
        return total.at[owner].add(expert_out * weight[:, None])

    total = lax.fori_loop(0, EXPERTS, add_expert, jnp.zeros((TOKENS, D), jnp.float32))
    combined = total.astype(jnp.bfloat16)
    return (combined, w_gate[partner], w_up[partner], w_down[partner],
            master_rows[partner], first_moment[partner], second_moment[partner])
```

```python
import functools

import jax
import jax.numpy as jnp
from jax import lax
from jax.experimental import pallas as pl
from jax.experimental.pallas import tpu as pltpu
from jax.sharding import PartitionSpec as P

MESH = pl.DeviceIdType.MESH
BF = jnp.bfloat16
F32 = jnp.float32

D = 3584
ACC = 32
CAP = 8
TOK = 128
NX, NY, NZ = 4, 4, 8
CH = NY * ACC
HALF = CH // 2
HID = 512
TILE = 512
NT = D // TILE


def rows_of(k, n=1):
    if isinstance(k, int):
        return pl.ds(k * CH, n * CH)
    return pl.ds(pl.multiple_of(k * CH, CH), n * CH)


def kernel(
    tok, acc, rt, gt, wg, wu, wd, ms, fm, sm,
    out, ng, nu, nd, nm, nf, nsd,
    w_g, w_u, w_d, gat, pck, rcv, ret, ring, fin, meta_y, meta, pick, wt_hi, wt_lo, hid,
    ys, yr, yms, ymr, zs, zr, zms, zmr, xs, xr, bs, br, is_, ir, fs, fr, ls, ws, wr, ms_s, ms_r,
):
    e = lax.axis_index("expert")
    q = lax.axis_index("zero")
    y, zh, x = e // 16, lax.rem(e // 4, 4), lax.rem(e, 4)
    zl, c = q // 2, lax.rem(q, 2)
    z = zh * 2 + zl

    def at(dy=0, dz=0, dx=0, dc=0):
        yy = lax.rem(y + dy + NY, NY)
        zz = lax.rem(z + dz + NZ, NZ)
        xx = lax.rem(x + dx + NX, NX)
        cc = lax.rem(c + dc, 2)
        return (yy * 16 + (zz // 2) * 4 + xx, lax.rem(zz, 2) * 2 + cc)

    def remote(src, dst, ssem, rsem, dev):
        return pltpu.make_async_remote_copy(src, dst, ssem, rsem, device_id=dev, device_id_type=MESH)

    barrier = pltpu.get_barrier_semaphore()
    peers = [at(dy=i) for i in (1, 2, 3)] + [at(dx=i) for i in (1, 2, 3)]
    peers += [at(dz=1), at(dz=-1), at(dc=1)]
    for dev in peers:
        pl.semaphore_signal(barrier, inc=1, device_id=dev, device_id_type=MESH)

    r128 = lax.broadcasted_iota(jnp.int32, (TOK, TOK), 0)
    c128 = lax.broadcasted_iota(jnp.int32, (TOK, TOK), 1)
    acc_row = acc[...].astype(F32)
    spread = jnp.broadcast_to(acc_row, (TOK, TOK))
    acc_col = jnp.sum(jnp.where(r128 == c128, spread, 0.0), axis=1, keepdims=True)
    rank_col = jnp.sum(jnp.where(c128 < r128, spread, 0.0), axis=1, keepdims=True)
    rank_row = jnp.sum(
        jnp.where(r128 < c128, jnp.broadcast_to(acc_col, (TOK, TOK)), 0.0), axis=0, keepdims=True
    )
    i32r = lax.broadcasted_iota(jnp.int32, (ACC, TOK), 0).astype(F32)
    sel = jnp.where((rank_row == i32r) & (acc_row > 0.5), 1.0, 0.0).astype(BF)
    pick[...] = sel
    my_rows = pl.ds(pl.multiple_of(y * ACC, ACC), ACC)
    for n in range(NT):
        cols = slice(n * TILE, (n + 1) * TILE)
        gat[my_rows, cols] = jnp.dot(sel, tok[:, cols], preferred_element_type=F32).astype(BF)
    lane = c128.astype(F32)
    sel2 = jnp.where((rank_col + (ACC * y).astype(F32) == lane) & (acc_col > 0.5), 1.0, 0.0).astype(BF)
    g_all = gt[...]
    g_hi = g_all.astype(BF).astype(F32)
    g_mid = (g_all - g_hi).astype(BF).astype(F32)
    g_lo = g_all - g_hi - g_mid
    stack = jnp.concatenate([rt[...].astype(F32), g_hi, g_mid, g_lo], axis=0).astype(BF)
    placed = jnp.dot(stack, sel2, preferred_element_type=F32)
    meta_y[0, 0:8, :] = placed[0:8]
    meta_y[0, 8:16, :] = placed[8:16] + placed[16:24] + placed[24:32]

    ring[rows_of(7), :] = jnp.zeros((CH, D), BF)
    ring[pl.ds(5 * CH + HALF, HALF), :] = jnp.zeros((HALF, D), BF)
    ring[pl.ds(6 * CH, HALF), :] = jnp.zeros((HALF, D), BF)

    pl.semaphore_wait(barrier, len(peers))

    y_copies = []
    for i in (1, 2, 3):
        dev = at(dy=i)
        y_copies.append(remote(gat.at[my_rows], gat.at[my_rows], ys.at[i - 1], yr.at[i - 1], dev))
        y_copies.append(remote(meta_y.at[0], meta_y.at[i], yms.at[i - 1], ymr.at[i - 1], dev))
    for cp in y_copies:
        cp.start()

    cols_c = pl.ds(pl.multiple_of(c * 256, 256), 256)
    w_pairs = [
        (wg.at[0], w_g.at[:, cols_c]),
        (wu.at[0], w_u.at[:, cols_c]),
        (wd.at[0], w_d.at[cols_c]),
    ]
    w_copies = []
    for i, (src, dst) in enumerate(w_pairs):
        w_copies.append(pltpu.make_async_copy(src, dst, ls.at[i]))
        w_copies.append(remote(src, dst, ws.at[i], wr.at[i], at(dc=1)))
    for cp in w_copies:
        cp.start()

    for i in (1, 2, 3):
        from_rows = pl.ds(pl.multiple_of(lax.rem(y - i + NY, NY) * ACC, ACC), ACC)
        remote(gat.at[from_rows], gat.at[from_rows], ys.at[i - 1], yr.at[i - 1], at(dy=-i)).wait_recv()
        remote(meta_y.at[0], meta_y.at[i], yms.at[i - 1], ymr.at[i - 1], at(dy=-i)).wait_recv()
    meta[0] = meta_y[0] + meta_y[1] + meta_y[2] + meta_y[3]

    def z_rows(src_k, dst_k, dz):
        return remote(gat.at[rows_of(src_k)], gat.at[rows_of(dst_k)], zs.at[dst_k], zr.at[dst_k], at(dz=dz))

    def z_meta(src_k, dst_k, dz):
        return remote(meta.at[src_k], meta.at[dst_k], zms.at[dst_k], zmr.at[dst_k], at(dz=dz))

    def z_half(which, dz):
        src = pl.ds((5 + which) * CH + which * HALF, HALF)
        dst = pl.ds(7 * CH + which * HALF, HALF)
        return remote(gat.at[src], gat.at[dst], zs.at[7 + which], zr.at[7 + which], at(dz=dz))

    for k, dz in ((1, 1), (2, -1)):
        z_rows(0, k, dz).start()
        z_meta(0, k, dz).start()

    m_copies = []
    for i, (src, dst) in enumerate(((wg, ng), (wu, nu), (wd, nd), (ms, nm), (fm, nf), (sm, nsd))):
        m_copies.append(remote(src, dst, ms_s.at[i], ms_r.at[i], at(dy=2)))
    for cp in m_copies:
        cp.start()

    base = (e - x).astype(F32)

    def x_send(k, i):
        r = pl.ds(k * CH + i * ACC, ACC) if isinstance(k, int) else pl.ds(pl.multiple_of(k * CH + i * ACC, ACC), ACC)
        return remote(pck.at[r], rcv.at[r], xs.at[k, i - 1], xr.at[k, i - 1], at(dx=i))

    def x_back(k, i):
        r = pl.ds(k * CH + i * ACC, ACC) if isinstance(k, int) else pl.ds(pl.multiple_of(k * CH + i * ACC, ACC), ACC)
        return remote(rcv.at[r], ret.at[r], bs.at[k, i - 1], br.at[k, i - 1], at(dx=-i))

    def pack(k):
        m = meta[k]
        routes, gates = m[0:8], m[8:16]
        i16 = lax.broadcasted_iota(jnp.int32, (16, CH), 0)
        want = base + lax.rem(x + i16, NX).astype(F32)
        hit = jnp.zeros((16, CH), F32)
        weight = jnp.zeros((16, CH), F32)
        for j in range(8):
            same = routes[j : j + 1] == want
            hit = hit + jnp.where(same, 1.0, 0.0)
            weight = weight + jnp.where(same, gates[j : j + 1], 0.0)
        group_r, group_c = r128 // ACC, c128 // ACC
        earlier = jnp.where((group_r == group_c) & (r128 < c128), 1.0, 0.0).astype(BF)
        rank = jnp.dot(hit.astype(BF), earlier, preferred_element_type=F32)
        lane_group = (lax.broadcasted_iota(jnp.int32, (16, CH), 1) // ACC).astype(F32)
        code = jnp.where(hit > 0.5, lane_group * CAP + rank, -1.0)
        ones, his, los = [], [], []
        for i in range(4):
            one = jnp.where(code[i : i + 1] == i32r, 1.0, 0.0)
            scaled = one * weight[i : i + 1]
            hi = scaled.astype(BF).astype(F32)
            ones.append(one)
            his.append(hi)
            los.append(scaled - hi)
        place = jnp.concatenate(ones, axis=0).astype(BF)
        wt_hi[k] = jnp.concatenate(his, axis=0).astype(BF)
        wt_lo[k] = jnp.concatenate(los, axis=0).astype(BF)
        first = k * CH if isinstance(k, int) else pl.multiple_of(k * CH, CH)

        @pl.loop(0, NT)
        def _(n):
            cols = pl.ds(pl.multiple_of(n * TILE, TILE), TILE)
            v = jnp.dot(place, gat[rows_of(k), cols], preferred_element_type=F32).astype(BF)
            rcv[pl.ds(first, ACC), cols] = v[:ACC]
            pck[pl.ds(first + ACC, CH - ACC), cols] = v[ACC:]

        for i in (1, 2, 3):
            x_send(k, i).start()

    def expert(k, n):
        for d in range(n):
            for i in (1, 2, 3):
                x_send(k + d, i).wait_recv()
        rows = rcv[rows_of(k, n), :]
        gate = jnp.dot(rows, w_g[...], preferred_element_type=F32)
        up = jnp.dot(rows, w_u[...], preferred_element_type=F32)
        hid[0 : n * CH, :] = (gate / (1.0 + jnp.exp(-gate)) * up).astype(BF)

        @pl.loop(0, NT)
        def _(t):
            cols = pl.ds(pl.multiple_of(t * TILE, TILE), TILE)
            v = jnp.dot(hid[0 : n * CH, :], w_d[:, cols], preferred_element_type=F32).astype(BF)
            rcv[rows_of(k, n), cols] = v
            for d in range(n):
                first = (k + d) * CH
                first = first if isinstance(first, int) else pl.multiple_of(first, CH)
                ret[pl.ds(first, ACC), cols] = v[d * CH : d * CH + ACC]

    def send_back(k):
        for i in (1, 2, 3):
            x_back(k, i).start()

    pack(0)
    for cp in w_copies[0::2]:
        cp.wait()
    for cp in w_copies[1::2]:
        cp.wait_recv()
    expert(0, 1)
    send_back(0)

    def step(s, carry):
        for k, dz in ((2 * s - 1, 1), (2 * s, -1)):
            z_rows(k, k, dz).wait_recv()
            z_meta(k, k, dz).wait_recv()

            @pl.when(s < 3)
            def _():
                z_rows(k, k + 2, dz).start()
                z_meta(k, k + 2, dz).start()

        @pl.when(s == 3)
        def _():
            z_half(0, 1).start()
            z_half(1, -1).start()
            z_meta(5, 7, 1).start()

        pack(2 * s - 1)
        pack(2 * s)

        @pl.when(s > 1)
        def _():
            expert(2 * s - 3, 2)

        return carry

    lax.fori_loop(1, 4, step, 0)
    z_half(0, 1).wait_recv()
    z_half(1, -1).wait_recv()
    z_meta(5, 7, 1).wait_recv()
    pack(7)
    expert(5, 2)
    expert(7, 1)
    send_back(7)
    send_back(6)

    def combine(k, slots):
        for i in (1, 2, 3):
            x_back(k, i).wait_recv()
        hi, lo = wt_hi[k], wt_lo[k]

        @pl.loop(0, NT)
        def _(n):
            cols = pl.ds(pl.multiple_of(n * TILE, TILE), TILE)
            part = ret[rows_of(k), cols]
            dims = (((0,), (0,)), ((), ()))
            v = lax.dot_general(hi, part, dims, preferred_element_type=F32)
            v = v + lax.dot_general(lo, part, dims, preferred_element_type=F32)
            for s in slots:
                v = v + ring[rows_of(s), cols].astype(F32)
            ring[rows_of(k), cols] = v.astype(BF)

    def r_rows(src_k, slot, dz):
        return remote(ring.at[rows_of(src_k)], ring.at[rows_of(slot)], is_.at[slot], ir.at[slot], at(dz=dz))

    def r_half(which, dz):
        src = pl.ds(7 * CH + which * HALF, HALF)
        dst = pl.ds((5 + which) * CH + which * HALF, HALF)
        return remote(ring.at[src], ring.at[dst], is_.at[5 + which], ir.at[5 + which], at(dz=dz))

    combine(7, (7,))
    r_half(0, -1).start()
    r_half(1, 1).start()

    def back(i, carry):
        s = 3 - i
        for k, dz in ((2 * s, 1), (2 * s - 1, -1)):

            @pl.when(k >= 2)
            def _():
                send_back(k - 1)

            @pl.when(s == 3)
            def _():
                r_half(1 if dz == 1 else 0, dz).wait_recv()

            @pl.when(s < 3)
            def _():
                r_rows(k, k, dz).wait_recv()

            combine(k, (k,))
            slot = jnp.where(k >= 3, k - 2, 0 if dz == -1 else 8)
            r_rows(k, slot, dz).start()
        return carry

    lax.fori_loop(0, 3, back, 0)
    r_rows(1, 0, -1).wait_recv()
    r_rows(2, 8, 1).wait_recv()
    combine(0, (0, 8))

    f_copies = []
    for i in (1, 2, 3):
        to_rows = pl.ds(pl.multiple_of(lax.rem(y + i, NY) * ACC, ACC), ACC)
        f_copies.append(remote(ring.at[to_rows], fin.at[i - 1], fs.at[i - 1], fr.at[i - 1], at(dy=i)))
    for cp in f_copies:
        cp.start()

    for cp in m_copies:
        cp.wait()
    for cp in w_copies[1::2]:
        cp.wait_send()
    for cp in y_copies:
        cp.wait_send()
    for k in range(1, 7):
        z_rows(0, k, 1).wait_send()
        z_meta(0, k, 1).wait_send()
    z_half(0, 1).wait_send()
    z_half(1, -1).wait_send()
    z_meta(5, 7, 1).wait_send()
    for k in range(8):
        for i in (1, 2, 3):
            x_send(k, i).wait_send()
            x_back(k, i).wait_send()
    r_half(0, -1).wait_send()
    r_half(1, 1).wait_send()
    for slot in (0, 1, 2, 3, 4, 8):
        r_rows(1, slot, 1).wait_send()

    for cp in f_copies:
        cp.wait()
    dims = (((0,), (0,)), ((), ()))
    for n in range(NT):
        cols = slice(n * TILE, (n + 1) * TILE)
        v = ring[my_rows, cols].astype(F32)
        for i in range(3):
            v = v + fin[i, :, cols].astype(F32)
        out[:, cols] = lax.dot_general(pick[...], v.astype(BF), dims, preferred_element_type=F32).astype(BF)


def on_device(tokens, accepted, routes, gates, partner, w_gate, w_up, w_down, master_rows, first_moment, second_moment):
    my_index = lax.axis_index("expert")
    ids = jnp.arange(partner.shape[0], dtype=jnp.int32)
    moving = jnp.sum(jnp.where(ids == my_index, partner, 0)) != my_index
    held = (w_gate, w_up, w_down, master_rows, first_moment, second_moment)
    vmem = pl.BlockSpec(memory_space=pltpu.VMEM)
    anywhere = pl.BlockSpec(memory_space=pl.ANY)
    dma = pltpu.SemaphoreType.DMA
    combined, *arrived = pl.pallas_call(
        kernel,
        out_shape=[jax.ShapeDtypeStruct(tokens.shape, BF)]
        + [jax.ShapeDtypeStruct(a.shape, a.dtype) for a in held],
        in_specs=[vmem] * 4 + [anywhere] * 6,
        out_specs=[vmem] + [anywhere] * 6,
        scratch_shapes=[
            pltpu.VMEM((D, HID), BF),
            pltpu.VMEM((D, HID), BF),
            pltpu.VMEM((HID, D), BF),
            pltpu.VMEM((8 * CH, D), BF),
            pltpu.VMEM((8 * CH, D), BF),
            pltpu.VMEM((8 * CH, D), BF),
            pltpu.VMEM((8 * CH, D), BF),
            pltpu.VMEM((9 * CH, D), BF),
            pltpu.VMEM((3, ACC, D), BF),
            pltpu.VMEM((4, 16, TOK), F32),
            pltpu.VMEM((8, 16, TOK), F32),
            pltpu.VMEM((ACC, TOK), BF),
            pltpu.VMEM((8, CH, CH), BF),
            pltpu.VMEM((8, CH, CH), BF),
            pltpu.VMEM((2 * CH, HID), BF),
            dma((3,)), dma((3,)), dma((3,)), dma((3,)),
            dma((9,)), dma((9,)), dma((8,)), dma((8,)),
            dma((8, 3)), dma((8, 3)), dma((8, 3)), dma((8, 3)),
            dma((9,)), dma((9,)),
            dma((3,)), dma((3,)),
            dma((3,)), dma((3,)), dma((3,)),
            dma((6,)), dma((6,)),
        ],
        compiler_params=pltpu.CompilerParams(
            collective_id=0, has_side_effects=True, vmem_limit_bytes=60 << 20
        ),
        cost_estimate=pl.CostEstimate(flops=12 * 1024 * D * HID, bytes_accessed=24 << 20, transcendentals=1024 * HID),
        name="experts",
    )(tokens, accepted.reshape(1, -1), routes.T, gates.T, *held)
    moved = tuple(jnp.where(moving, new, old) for new, old in zip(arrived, held))
    return (combined,) + moved


def solution(mesh):
    both = P(("expert", "zero"), None)
    cols = P("expert", None, "zero")
    rows = P("expert", "zero", None)
    return jax.shard_map(
        on_device,
        mesh=mesh,
        in_specs=(both, P(("expert", "zero")), both, both, P(), cols, cols, rows, rows, rows, rows),
        out_specs=(both, cols, cols, rows, rows, rows, rows),
        check_vma=False,
    )
```

```python
import functools

import jax
import jax.numpy as jnp
from jax import lax
from jax.experimental import pallas as pl
from jax.experimental.pallas import tpu as pltpu
from jax.sharding import PartitionSpec as P

MESH = pl.DeviceIdType.MESH
BF = jnp.bfloat16
F32 = jnp.float32

D = 3584
ACC = 32
CAP = 8
TOK = 128
NX, NY, NZ = 4, 4, 8
UNIT = 2 * ACC
GROUP = UNIT // 4
OWN = 7
HID = 512
TILE = 512
NT = D // TILE


def unit_rows(w, p, first=0, count=UNIT):
    if isinstance(w, int) and isinstance(p, int):
        return pl.ds((w * 8 + p) * UNIT + first, count)
    return pl.ds(pl.multiple_of((w * 8 + p) * UNIT + first, 16), count)


def ring_rows(w, slot, first=0, count=UNIT):
    if isinstance(w, int) and isinstance(slot, int):
        return pl.ds((w * 9 + slot) * UNIT + first, count)
    return pl.ds(pl.multiple_of((w * 9 + slot) * UNIT + first, 16), count)


def kernel(
    tok, acc, rt, gt, wg, wu, wd, ms, fm, sm,
    out, ng, nu, nd, nm, nf, nsd,
    w_g, w_u, w_d, gat, pck, rcv, ret, ring, fin, meta_y, meta_in, meta, pick, wt_hi, wt_lo, hid,
    ys, yr, yms, ymr, zs, zr, zms, zmr, xs, xr, bs, br, is_, ir, fs, fr, ls, ws, wr, ms_s, ms_r,
):
    e = lax.axis_index("expert")
    q = lax.axis_index("zero")
    y, zh, x = e // 16, lax.rem(e // 4, 4), lax.rem(e, 4)
    zl, c = q // 2, lax.rem(q, 2)
    z = zh * 2 + zl

    def at(dy=0, dz=0, dx=0, dc=0):
        yy = lax.rem(y + dy + NY, NY)
        zz = lax.rem(z + dz + NZ, NZ)
        xx = lax.rem(x + dx + NX, NX)
        cc = lax.rem(c + dc, 2)
        return (yy * 16 + (zz // 2) * 4 + xx, lax.rem(zz, 2) * 2 + cc)

    def remote(src, dst, ssem, rsem, dev):
        return pltpu.make_async_remote_copy(src, dst, ssem, rsem, device_id=dev, device_id_type=MESH)

    barrier = pltpu.get_barrier_semaphore()
    peers = [at(dy=i) for i in (1, 2, 3)] + [at(dx=i) for i in (1, 2, 3)]
    peers += [at(dz=1), at(dz=-1), at(dc=1)]
    for dev in peers:
        pl.semaphore_signal(barrier, inc=1, device_id=dev, device_id_type=MESH)

    r128 = lax.broadcasted_iota(jnp.int32, (TOK, TOK), 0)
    c128 = lax.broadcasted_iota(jnp.int32, (TOK, TOK), 1)
    acc_row = acc[...].astype(F32)
    spread = jnp.broadcast_to(acc_row, (TOK, TOK))
    acc_col = jnp.sum(jnp.where(r128 == c128, spread, 0.0), axis=1, keepdims=True)
    rank_col = jnp.sum(jnp.where(c128 < r128, spread, 0.0), axis=1, keepdims=True)
    rank_row = jnp.sum(
        jnp.where(r128 < c128, jnp.broadcast_to(acc_col, (TOK, TOK)), 0.0), axis=0, keepdims=True
    )
    i32r = lax.broadcasted_iota(jnp.int32, (ACC, TOK), 0).astype(F32)
    sel = jnp.where((rank_row == i32r) & (acc_row > 0.5), 1.0, 0.0).astype(BF)
    pick[...] = sel
    own_block = unit_rows(0, OWN, 0, ACC)
    for n in range(NT):
        cols = slice(n * TILE, (n + 1) * TILE)
        gat[own_block, cols] = jnp.dot(sel, tok[:, cols], preferred_element_type=F32).astype(BF)
    wide = lax.broadcasted_iota(jnp.int32, (TOK, NY * TOK), 1)
    offset = (wide // TOK) * (TOK + ACC)
    here = (rank_col + offset.astype(F32) == wide.astype(F32)) & (acc_col > 0.5)
    sel2 = jnp.where(here, 1.0, 0.0).astype(BF)
    g_all = gt[...]
    g_hi = g_all.astype(BF).astype(F32)
    g_mid = (g_all - g_hi).astype(BF).astype(F32)
    g_lo = g_all - g_hi - g_mid
    stack = jnp.concatenate([rt[...].astype(F32), g_hi, g_mid, g_lo], axis=0).astype(BF)
    placed = jnp.dot(stack, sel2, preferred_element_type=F32)
    for j in range(NY):
        part = placed[:, j * TOK : (j + 1) * TOK]
        meta_y[j, 0:8, :] = part[0:8]
        meta_y[j, 8:16, :] = part[8:16] + part[16:24] + part[24:32]

    for w in range(2):
        ring[ring_rows(w, 6), :] = jnp.zeros((UNIT, D), BF)
        ring[ring_rows(w, 4, ACC, ACC), :] = jnp.zeros((ACC, D), BF)
        ring[ring_rows(w, 5, 0, ACC), :] = jnp.zeros((ACC, D), BF)

    pl.semaphore_wait(barrier, len(peers))

    y_copies = []
    for i in (3, 2, 1):
        dev, j = at(dy=i), NY - i
        dst = unit_rows(j // 2, OWN, (j % 2) * ACC, ACC)
        y_copies.append(remote(meta_y.at[j], meta_in.at[j - 1], yms.at[j - 1], ymr.at[j - 1], dev))
        y_copies.append(remote(gat.at[own_block], gat.at[dst], ys.at[j - 1], yr.at[j - 1], dev))
    for cp in y_copies:
        cp.start()

    cols_c = pl.ds(pl.multiple_of(c * 256, 256), 256)
    w_pairs = [
        (wg.at[0], w_g.at[:, cols_c]),
        (wu.at[0], w_u.at[:, cols_c]),
        (wd.at[0], w_d.at[cols_c]),
    ]
    w_copies = []
    for i, (src, dst) in enumerate(w_pairs):
        w_copies.append(pltpu.make_async_copy(src, dst, ls.at[i]))
        w_copies.append(remote(src, dst, ws.at[i], wr.at[i], at(dc=1)))
    for cp in w_copies:
        cp.start()

    def z_rows(w, p, to, dz):
        return remote(gat.at[unit_rows(w, p)], gat.at[unit_rows(w, to)], zs.at[w, to], zr.at[w, to], at(dz=dz))

    def z_half(w, h):
        src, dst = unit_rows(w, 4 + h, h * ACC, ACC), unit_rows(w, 6, h * ACC, ACC)
        return remote(gat.at[src], gat.at[dst], zs.at[w, 6 + h], zr.at[w, 6 + h], at(dz=1 - 2 * h))

    def z_meta(p, to, dz):
        return remote(meta.at[p], meta.at[to], zms.at[to], zmr.at[to], at(dz=dz))

    def z_block(b, to, dz):
        src, dst = unit_rows(0, OWN, b * ACC, ACC), unit_rows(0, to, b * ACC, ACC)
        n = to if b == 0 else 8 + to
        return remote(gat.at[src], gat.at[dst], zs.at[0, n], zr.at[0, n], at(dz=dz))

    z_block(0, 0, 1).start()
    z_block(0, 1, -1).start()
    for i in range(0, 6, 2):
        y_copies[i].wait_recv()
    meta[OWN] = meta_y[0] + meta_in[0] + meta_in[1] + meta_in[2]
    z_meta(OWN, 0, 1).start()
    z_meta(OWN, 1, -1).start()
    y_copies[1].wait_recv()
    z_block(1, 0, 1).start()
    z_block(1, 1, -1).start()

    base = (e - x).astype(F32)

    def x_send(w, p, i):
        r = unit_rows(w, p, i * GROUP, GROUP)
        return remote(pck.at[r], rcv.at[r], xs.at[w * 8 + p, i - 1], xr.at[w * 8 + p, i - 1], at(dx=i))

    def x_back(w, p, i):
        r = unit_rows(w, p, i * GROUP, GROUP)
        return remote(rcv.at[r], ret.at[r], bs.at[w * 8 + p, i - 1], br.at[w * 8 + p, i - 1], at(dx=-i))

    def pack(w, p):
        m = meta[p]
        m = jnp.where(w == 0, m, pltpu.roll(m, UNIT, 1))
        routes, gates = m[0:8], m[8:16]
        i16 = lax.broadcasted_iota(jnp.int32, (16, TOK), 0)
        want = base + lax.rem(x + i16, NX).astype(F32)
        hit = jnp.zeros((16, TOK), F32)
        weight = jnp.zeros((16, TOK), F32)
        for j in range(8):
            same = routes[j : j + 1] == want
            hit = hit + jnp.where(same, 1.0, 0.0)
            weight = weight + jnp.where(same, gates[j : j + 1], 0.0)
        earlier = jnp.where((r128 // ACC == c128 // ACC) & (r128 < c128), 1.0, 0.0).astype(BF)
        rank = jnp.dot(hit.astype(BF), earlier, preferred_element_type=F32)
        lane_group = (lax.broadcasted_iota(jnp.int32, (16, TOK), 1) // ACC).astype(F32)
        code = jnp.where(hit > 0.5, lane_group * CAP + rank, -1.0)
        ones, his, los = [], [], []
        for i in range(4):
            one = jnp.where(code[i : i + 1] == i32r[0:GROUP], 1.0, 0.0)
            scaled = one * weight[i : i + 1]
            hi = scaled.astype(BF).astype(F32)
            ones.append(one)
            his.append(hi)
            los.append(scaled - hi)
        place = jnp.concatenate(ones, axis=0).astype(BF)[:, 0:UNIT]
        wt_hi[w * 8 + p] = jnp.concatenate(his, axis=0).astype(BF)
        wt_lo[w * 8 + p] = jnp.concatenate(los, axis=0).astype(BF)

        @pl.loop(0, NT)
        def _(n):
            cols = pl.ds(pl.multiple_of(n * TILE, TILE), TILE)
            v = jnp.dot(place, gat[unit_rows(w, p), cols], preferred_element_type=F32).astype(BF)
            rcv[unit_rows(w, p, 0, GROUP), cols] = v[:GROUP]
            pck[unit_rows(w, p, GROUP, UNIT - GROUP), cols] = v[GROUP:]

        for i in (1, 2, 3):
            x_send(w, p, i).start()

    def expert(w, p):
        for d in range(2):
            for i in (1, 2, 3):
                x_send(w, p + d, i).wait_recv()
        rows = rcv[unit_rows(w, p, 0, 2 * UNIT), :]
        gate = jnp.dot(rows, w_g[...], preferred_element_type=F32)
        up = jnp.dot(rows, w_u[...], preferred_element_type=F32)
        hid[...] = (gate / (1.0 + jnp.exp(-gate)) * up).astype(BF)

        @pl.loop(0, NT)
        def _(t):
            cols = pl.ds(pl.multiple_of(t * TILE, TILE), TILE)
            v = jnp.dot(hid[...], w_d[:, cols], preferred_element_type=F32).astype(BF)
            rcv[unit_rows(w, p, 0, 2 * UNIT), cols] = v
            for d in range(2):
                ret[unit_rows(w, p + d, 0, GROUP), cols] = v[d * UNIT : d * UNIT + GROUP]

    def send_back(w, p):
        for i in (1, 2, 3):
            x_back(w, p, i).start()

    def combine(w, p, slots):
        for i in (1, 2, 3):
            x_back(w, p, i).wait_recv()
        hi, lo = wt_hi[w * 8 + p][:, 0:UNIT], wt_lo[w * 8 + p][:, 0:UNIT]

        @pl.loop(0, NT)
        def _(n):
            cols = pl.ds(pl.multiple_of(n * TILE, TILE), TILE)
            part = ret[unit_rows(w, p), cols]
            dims = (((0,), (0,)), ((), ()))
            v = lax.dot_general(hi, part, dims, preferred_element_type=F32)
            v = v + lax.dot_general(lo, part, dims, preferred_element_type=F32)
            for s in slots:
                v = v + ring[ring_rows(w, s), cols].astype(F32)
            ring[ring_rows(w, slots[0]), cols] = v.astype(BF)

    def r_rows(w, p, to, dz):
        return remote(ring.at[ring_rows(w, p)], ring.at[ring_rows(w, to)], is_.at[w, to], ir.at[w, to], at(dz=dz))

    def r_half(w, h):
        src, dst = ring_rows(w, 6, h * ACC, ACC), ring_rows(w, 4 + h, h * ACC, ACC)
        return remote(ring.at[src], ring.at[dst], is_.at[w, 4 + h], ir.at[w, 4 + h], at(dz=2 * h - 1))

    def y_sum(j):
        src = ring_rows(j // 2, OWN, (j % 2) * ACC, ACC)
        return remote(ring.at[src], fin.at[j - 1], fs.at[j - 1], fr.at[j - 1], at(dy=j))

    pack(0, OWN)

    m_copies = []
    for i, (src, dst) in enumerate(((wg, ng), (wu, nu), (wd, nd), (ms, nm), (fm, nf), (sm, nsd))):
        m_copies.append(remote(src, dst, ms_s.at[i], ms_r.at[i], at(dy=2)))
    for cp in m_copies:
        cp.start()

    y_copies[3].wait_recv()
    y_copies[5].wait_recv()
    pack(1, OWN)
    for cp in w_copies[0::2]:
        cp.wait()
    for cp in w_copies[1::2]:
        cp.wait_recv()

    def tick(i, carry):
        w = jnp.where(i > 4, 1, 0)
        s = i - 4 * w
        first = 2 * s - 2

        @pl.when((i <= 8) & (s <= 3))
        def _():
            for h in range(2):
                dz = 1 - 2 * h

                @pl.when(i == 1)
                def _():
                    z_block(0, h, dz).wait_recv()
                    z_block(1, h, dz).wait_recv()

                @pl.when(i > 1)
                def _():
                    z_rows(w, first + h, first + h, dz).wait_recv()

                @pl.when(s < 3)
                def _():
                    z_rows(w, first + h, first + h + 2, dz).start()

                @pl.when(s == 3)
                def _():
                    z_half(w, h).start()

            @pl.when(i == 3)
            def _():
                z_rows(1, OWN, 0, 1).start()
                z_rows(1, OWN, 1, -1).start()

            @pl.when(i <= 3)
            def _():
                for h in range(2):
                    dz = 1 - 2 * h
                    z_meta(first + h, first + h, dz).wait_recv()

                    @pl.when(s < 3)
                    def _():
                        z_meta(first + h, first + h + 2, dz).start()

                @pl.when(s == 3)
                def _():
                    z_meta(4, 6, 1).start()

        @pl.when((i <= 8) & (s == 4))
        def _():
            z_half(w, 0).wait_recv()
            z_half(w, 1).wait_recv()

            @pl.when(i == 4)
            def _():
                z_meta(4, 6, 1).wait_recv()

        @pl.when(i <= 8)
        def _():
            @pl.loop(0, jnp.where(s == 4, 1, 2))
            def _(d):
                pack(w, first + d)

        @pl.when(i >= 9)
        def _():
            send_back_step(i - 9)

        @pl.when(i >= 3)
        def _():
            we = jnp.where(i > 6, 1, 0)
            expert(we, 2 * (i - 2 - 4 * we) - 2)

        return carry

    def wave_and_distance(r):
        w = jnp.where(r < 4, r // 2, lax.rem(r, 2))
        return w, jnp.where(r < 4, 4 - lax.rem(r, 2), 4 - r // 2)

    def send_back_step(r):
        w, s = wave_and_distance(r)

        @pl.when((r < 8) & (s == 4))
        def _():
            send_back(w, 6)

        @pl.when((r < 8) & (s < 4))
        def _():
            send_back(w, 2 * s - 1)
            send_back(w, 2 * s - 2)

        @pl.when(r >= 8)
        def _():
            send_back(r - 8, OWN)

    def return_step(r, carry):
        w, s = wave_and_distance(r)
        send_back_step(r + 2)

        @pl.when(s == 4)
        def _():
            combine(w, 6, (6,))
            r_half(w, 0).start()
            r_half(w, 1).start()

        @pl.when(s < 4)
        def _():
            @pl.loop(0, 2)
            def _(h):
                p = 2 * s - 1 - h
                dz = 1 - 2 * h

                @pl.when(s == 3)
                def _():
                    r_half(w, 1 - h).wait_recv()

                @pl.when(s < 3)
                def _():
                    r_rows(w, p, p, dz).wait_recv()

                combine(w, p, (p,))
                r_rows(w, p, jnp.where(p >= 2, p - 2, OWN + p), dz).start()

        return carry

    lax.fori_loop(1, 11, tick, 0)
    lax.fori_loop(0, 8, return_step, 0)

    @pl.loop(0, 2)
    def _(w):
        r_rows(w, 0, OWN, -1).wait_recv()
        r_rows(w, 1, OWN + 1, 1).wait_recv()
        combine(w, OWN, (OWN, OWN + 1))

        @pl.when(w == 0)
        def _():
            y_sum(1).start()

    y_sum(2).start()
    y_sum(3).start()

    for cp in m_copies:
        cp.wait()
    for cp in w_copies[1::2]:
        cp.wait_send()
    for cp in y_copies:
        cp.wait_send()
    for p in range(7):
        z_meta(OWN, p, 1).wait_send()
    for p in range(2):
        z_rows(1, OWN, p, 1).wait_send()
        for b in range(2):
            z_block(b, p, 1).wait_send()

    @pl.loop(0, 2)
    def _(w):
        for p in range(2, 6):
            z_rows(w, OWN, p, 1).wait_send()
        for h in range(2):
            z_half(w, h).wait_send()
            r_half(w, h).wait_send()
        for slot in (0, 1, 2, 3, OWN, OWN + 1):
            r_rows(w, 0, slot, 1).wait_send()

        @pl.loop(0, 8)
        def _(p):
            for i in (1, 2, 3):
                x_send(w, p, i).wait_send()
                x_back(w, p, i).wait_send()

    for j in (1, 2, 3):
        y_sum(j).wait()
    dims = (((0,), (0,)), ((), ()))
    for n in range(NT):
        cols = slice(n * TILE, (n + 1) * TILE)
        v = ring[ring_rows(0, OWN, 0, ACC), cols].astype(F32)
        for i in range(3):
            v = v + fin[i, :, cols].astype(F32)
        out[:, cols] = lax.dot_general(pick[...], v.astype(BF), dims, preferred_element_type=F32).astype(BF)


def on_device(tokens, accepted, routes, gates, partner, w_gate, w_up, w_down, master_rows, first_moment, second_moment):
    my_index = lax.axis_index("expert")
    ids = jnp.arange(partner.shape[0], dtype=jnp.int32)
    moving = jnp.sum(jnp.where(ids == my_index, partner, 0)) != my_index
    held = (w_gate, w_up, w_down, master_rows, first_moment, second_moment)
    vmem = pl.BlockSpec(memory_space=pltpu.VMEM)
    anywhere = pl.BlockSpec(memory_space=pl.ANY)
    dma = pltpu.SemaphoreType.DMA
    combined, *arrived = pl.pallas_call(
        kernel,
        out_shape=[jax.ShapeDtypeStruct(tokens.shape, BF)]
        + [jax.ShapeDtypeStruct(a.shape, a.dtype) for a in held],
        in_specs=[vmem] * 4 + [anywhere] * 6,
        out_specs=[vmem] + [anywhere] * 6,
        scratch_shapes=[
            pltpu.VMEM((D, HID), BF),
            pltpu.VMEM((D, HID), BF),
            pltpu.VMEM((HID, D), BF),
            pltpu.VMEM((16 * UNIT, D), BF),
            pltpu.VMEM((16 * UNIT, D), BF),
            pltpu.VMEM((16 * UNIT, D), BF),
            pltpu.VMEM((16 * UNIT, D), BF),
            pltpu.VMEM((18 * UNIT, D), BF),
            pltpu.VMEM((3, ACC, D), BF),
            pltpu.VMEM((4, 16, TOK), F32),
            pltpu.VMEM((3, 16, TOK), F32),
            pltpu.VMEM((8, 16, TOK), F32),
            pltpu.VMEM((ACC, TOK), BF),
            pltpu.VMEM((16, UNIT, TOK), BF),
            pltpu.VMEM((16, UNIT, TOK), BF),
            pltpu.VMEM((2 * UNIT, HID), BF),
            dma((3,)), dma((3,)), dma((3,)), dma((3,)),
            dma((2, 10)), dma((2, 10)), dma((7,)), dma((7,)),
            dma((16, 3)), dma((16, 3)), dma((16, 3)), dma((16, 3)),
            dma((2, 9)), dma((2, 9)),
            dma((3,)), dma((3,)),
            dma((3,)), dma((3,)), dma((3,)),
            dma((6,)), dma((6,)),
        ],
        compiler_params=pltpu.CompilerParams(
            collective_id=0, has_side_effects=True, vmem_limit_bytes=60 << 20
        ),
        cost_estimate=pl.CostEstimate(flops=12 * 1024 * D * HID, bytes_accessed=24 << 20, transcendentals=1024 * HID),
        name="experts",
    )(tokens, accepted.reshape(1, -1), routes.T, gates.T, *held)
    moved = [jnp.where(moving, new, old) for new, old in zip(arrived, held)]
    return (combined, *moved)


def solution(mesh):
    both = P(("expert", "zero"), None)
    cols = P("expert", None, "zero")
    rows = P("expert", "zero", None)
    return jax.shard_map(
        on_device,
        mesh=mesh,
        in_specs=(both, P(("expert", "zero")), both, both, P(), cols, cols, rows, rows, rows, rows),
        out_specs=(both, cols, cols, rows, rows, rows, rows),
        check_vma=False,
    )
```

```python
import functools

import jax
import jax.numpy as jnp
from jax import lax
from jax.experimental import pallas as pl
from jax.experimental.pallas import tpu as pltpu
from jax.sharding import PartitionSpec as P

MESH = pl.DeviceIdType.MESH
BF = jnp.bfloat16
F32 = jnp.float32

D = 3584
ACC = 32
CAP = 8
TOK = 128
NX, NY, NZ = 4, 4, 8
UNIT = 2 * ACC
GROUP = UNIT // 4
OWN = 7
STEP = (0, 2, 1, 3)
HID = 512
TILE = 1792
NT = D // TILE


def unit_rows(w, p, first=0, count=UNIT):
    if isinstance(w, int) and isinstance(p, int):
        return pl.ds((w * 8 + p) * UNIT + first, count)
    return pl.ds(pl.multiple_of((w * 8 + p) * UNIT + first, 16), count)


def ring_rows(w, slot, first=0, count=UNIT):
    if isinstance(w, int) and isinstance(slot, int):
        return pl.ds((w * 9 + slot) * UNIT + first, count)
    return pl.ds(pl.multiple_of((w * 9 + slot) * UNIT + first, 16), count)


def kernel(
    tok, acc, rt, gt, wg, wu, wd, ms, fm, sm,
    out, ng, nu, nd, nm, nf, nsd,
    w_g, w_u, w_d, gat, pck, rcv, ret, ring, fin, meta_y, meta_in, meta, pick, wt_hi, wt_lo, hid,
    ys, yr, yms, ymr, zs, zr, zms, zmr, xs, xr, bs, br, is_, ir, fs, fr, ls, ws, wr, ms_s, ms_r,
):
    e = lax.axis_index("expert")
    q = lax.axis_index("zero")
    y, zh, x = e // 16, lax.rem(e // 4, 4), lax.rem(e, 4)
    zl, c = q // 2, lax.rem(q, 2)
    z = zh * 2 + zl

    def at(dy=0, dz=0, dx=0, dc=0):
        yy = lax.rem(y + dy + NY, NY)
        zz = lax.rem(z + dz + NZ, NZ)
        xx = lax.rem(x + dx + NX, NX)
        cc = lax.rem(c + dc, 2)
        return (yy * 16 + (zz // 2) * 4 + xx, lax.rem(zz, 2) * 2 + cc)

    def remote(src, dst, ssem, rsem, dev):
        return pltpu.make_async_remote_copy(src, dst, ssem, rsem, device_id=dev, device_id_type=MESH)

    barrier = pltpu.get_barrier_semaphore()
    peers = [at(dy=i) for i in (1, 2, 3)] + [at(dx=i) for i in (1, 2, 3)]
    peers += [at(dz=1), at(dz=-1), at(dc=1)]
    for dev in peers:
        pl.semaphore_signal(barrier, inc=1, device_id=dev, device_id_type=MESH)

    r128 = lax.broadcasted_iota(jnp.int32, (TOK, TOK), 0)
    c128 = lax.broadcasted_iota(jnp.int32, (TOK, TOK), 1)
    acc_row = acc[...].astype(F32)
    spread = jnp.broadcast_to(acc_row, (TOK, TOK))
    acc_col = jnp.sum(jnp.where(r128 == c128, spread, 0.0), axis=1, keepdims=True)
    rank_col = jnp.sum(jnp.where(c128 < r128, spread, 0.0), axis=1, keepdims=True)
    rank_row = jnp.sum(
        jnp.where(r128 < c128, jnp.broadcast_to(acc_col, (TOK, TOK)), 0.0), axis=0, keepdims=True
    )
    i32r = lax.broadcasted_iota(jnp.int32, (ACC, TOK), 0).astype(F32)
    sel = jnp.where((rank_row == i32r) & (acc_row > 0.5), 1.0, 0.0).astype(BF)
    pick[...] = sel
    own_block = unit_rows(0, OWN, 0, ACC)
    for n in range(NT):
        cols = slice(n * TILE, (n + 1) * TILE)
        gat[own_block, cols] = jnp.dot(sel, tok[:, cols], preferred_element_type=F32).astype(BF)
    wide = lax.broadcasted_iota(jnp.int32, (TOK, NY * TOK), 1)
    offset = (wide // TOK) * (TOK + ACC)
    here = (rank_col + offset.astype(F32) == wide.astype(F32)) & (acc_col > 0.5)
    sel2 = jnp.where(here, 1.0, 0.0).astype(BF)
    g_all = gt[...]
    g_hi = g_all.astype(BF).astype(F32)
    g_mid = (g_all - g_hi).astype(BF).astype(F32)
    g_lo = g_all - g_hi - g_mid
    stack = jnp.concatenate([rt[...].astype(F32), g_hi, g_mid, g_lo], axis=0).astype(BF)
    placed = jnp.dot(stack, sel2, preferred_element_type=F32)
    for j in range(NY):
        part = placed[:, j * TOK : (j + 1) * TOK]
        meta_y[j, 0:8, :] = part[0:8]
        meta_y[j, 8:16, :] = part[8:16] + part[16:24] + part[24:32]

    for w in range(2):
        ring[ring_rows(w, 6), :] = jnp.zeros((UNIT, D), BF)
        ring[ring_rows(w, 4, ACC, ACC), :] = jnp.zeros((ACC, D), BF)
        ring[ring_rows(w, 5, 0, ACC), :] = jnp.zeros((ACC, D), BF)

    pl.semaphore_wait(barrier, len(peers))

    y_meta, y_rows = [], []
    for n in (1, 2, 3):
        dev = at(dy=-STEP[n])
        dst = unit_rows(n // 2, OWN, (n % 2) * ACC, ACC)
        y_meta.append(remote(meta_y.at[n], meta_in.at[n - 1], yms.at[n - 1], ymr.at[n - 1], dev))
        y_rows.append(remote(gat.at[own_block], gat.at[dst], ys.at[n - 1], yr.at[n - 1], dev))
    y_rows[0].start()
    for cp in y_meta:
        cp.start()

    cols_c = pl.ds(pl.multiple_of(c * 256, 256), 256)
    w_pairs = [
        (wg.at[0], w_g.at[:, cols_c]),
        (wu.at[0], w_u.at[:, cols_c]),
        (wd.at[0], w_d.at[cols_c]),
    ]
    w_copies = []
    for i, (src, dst) in enumerate(w_pairs):
        w_copies.append(pltpu.make_async_copy(src, dst, ls.at[i]))
        w_copies.append(remote(src, dst, ws.at[i], wr.at[i], at(dc=1)))
    for cp in w_copies:
        cp.start()

    def z_rows(w, p, to, dz):
        return remote(gat.at[unit_rows(w, p)], gat.at[unit_rows(w, to)], zs.at[w, to], zr.at[w, to], at(dz=dz))

    def z_half(w, h):
        src, dst = unit_rows(w, 4 + h, h * ACC, ACC), unit_rows(w, 6, h * ACC, ACC)
        return remote(gat.at[src], gat.at[dst], zs.at[w, 6 + h], zr.at[w, 6 + h], at(dz=1 - 2 * h))

    def z_meta(p, to, dz):
        return remote(meta.at[p], meta.at[to], zms.at[to], zmr.at[to], at(dz=dz))

    def z_block(b, to, dz):
        src, dst = unit_rows(0, OWN, b * ACC, ACC), unit_rows(0, to, b * ACC, ACC)
        n = to if b == 0 else 8 + to
        return remote(gat.at[src], gat.at[dst], zs.at[0, n], zr.at[0, n], at(dz=dz))

    z_block(0, 0, 1).start()
    z_block(0, 1, -1).start()
    for cp in y_meta:
        cp.wait_recv()
    meta[OWN] = meta_y[0] + meta_in[0] + meta_in[1] + meta_in[2]
    z_meta(OWN, 0, 1).start()
    z_meta(OWN, 1, -1).start()
    y_rows[0].wait_recv()
    z_block(1, 0, 1).start()
    z_block(1, 1, -1).start()
    for cp in y_rows[1:]:
        cp.start()

    base = (e - x).astype(F32)

    def x_send(w, p, i):
        r = unit_rows(w, p, i * GROUP, GROUP)
        return remote(pck.at[r], rcv.at[r], xs.at[w * 8 + p, i - 1], xr.at[w * 8 + p, i - 1], at(dx=i))

    def x_back(w, p, i):
        r = unit_rows(w, p, i * GROUP, GROUP)
        return remote(rcv.at[r], ret.at[r], bs.at[w * 8 + p, i - 1], br.at[w * 8 + p, i - 1], at(dx=-i))

    def pack(w, p):
        m = meta[p]
        m = jnp.where(w == 0, m, pltpu.roll(m, UNIT, 1))
        routes, gates = m[0:8], m[8:16]
        i16 = lax.broadcasted_iota(jnp.int32, (16, TOK), 0)
        want = base + lax.rem(x + i16, NX).astype(F32)
        hit = jnp.zeros((16, TOK), F32)
        weight = jnp.zeros((16, TOK), F32)
        for j in range(8):
            same = routes[j : j + 1] == want
            hit = hit + jnp.where(same, 1.0, 0.0)
            weight = weight + jnp.where(same, gates[j : j + 1], 0.0)
        earlier = jnp.where((r128 // ACC == c128 // ACC) & (r128 < c128), 1.0, 0.0).astype(BF)
        rank = jnp.dot(hit.astype(BF), earlier, preferred_element_type=F32)
        lane_group = (lax.broadcasted_iota(jnp.int32, (16, TOK), 1) // ACC).astype(F32)
        code = jnp.where(hit > 0.5, lane_group * CAP + rank, -1.0)
        ones, his, los = [], [], []
        for i in range(4):
            one = jnp.where(code[i : i + 1] == i32r[0:GROUP], 1.0, 0.0)
            scaled = one * weight[i : i + 1]
            hi = scaled.astype(BF).astype(F32)
            ones.append(one)
            his.append(hi)
            los.append(scaled - hi)
        place = jnp.concatenate(ones, axis=0).astype(BF)[:, 0:UNIT]
        wt_hi[w * 8 + p] = jnp.concatenate(his, axis=0).astype(BF)
        wt_lo[w * 8 + p] = jnp.concatenate(los, axis=0).astype(BF)

        @pl.loop(0, NT)
        def _(n):
            cols = pl.ds(pl.multiple_of(n * TILE, TILE), TILE)
            v = jnp.dot(place, gat[unit_rows(w, p), cols], preferred_element_type=F32).astype(BF)
            rcv[unit_rows(w, p, 0, GROUP), cols] = v[:GROUP]
            pck[unit_rows(w, p, GROUP, UNIT - GROUP), cols] = v[GROUP:]

        for i in (1, 2, 3):
            x_send(w, p, i).start()

    def expert(w, p):
        for d in range(2):
            for i in (1, 2, 3):
                x_send(w, p + d, i).wait_recv()
        rows = rcv[unit_rows(w, p, 0, 2 * UNIT), :]
        gate = jnp.dot(rows, w_g[...], preferred_element_type=F32)
        up = jnp.dot(rows, w_u[...], preferred_element_type=F32)
        hid[...] = (gate / (1.0 + jnp.exp(-gate)) * up).astype(BF)

        @pl.loop(0, NT)
        def _(t):
            cols = pl.ds(pl.multiple_of(t * TILE, TILE), TILE)
            v = jnp.dot(hid[...], w_d[:, cols], preferred_element_type=F32).astype(BF)
            rcv[unit_rows(w, p, 0, 2 * UNIT), cols] = v
            for d in range(2):
                ret[unit_rows(w, p + d, 0, GROUP), cols] = v[d * UNIT : d * UNIT + GROUP]

    def send_back(w, p):
        for i in (1, 2, 3):
            x_back(w, p, i).start()

    def combine(w, p, slots):
        for i in (1, 2, 3):
            x_back(w, p, i).wait_recv()
        hi, lo = wt_hi[w * 8 + p][:, 0:UNIT], wt_lo[w * 8 + p][:, 0:UNIT]

        @pl.loop(0, NT)
        def _(n):
            cols = pl.ds(pl.multiple_of(n * TILE, TILE), TILE)
            part = ret[unit_rows(w, p), cols]
            dims = (((0,), (0,)), ((), ()))
            v = lax.dot_general(hi, part, dims, preferred_element_type=F32)
            v = v + lax.dot_general(lo, part, dims, preferred_element_type=F32)
            for s in slots:
                v = v + ring[ring_rows(w, s), cols].astype(F32)
            ring[ring_rows(w, slots[0]), cols] = v.astype(BF)

    def r_rows(w, p, to, dz):
        return remote(ring.at[ring_rows(w, p)], ring.at[ring_rows(w, to)], is_.at[w, to], ir.at[w, to], at(dz=dz))

    def r_half(w, h):
        src, dst = ring_rows(w, 6, h * ACC, ACC), ring_rows(w, 4 + h, h * ACC, ACC)
        return remote(ring.at[src], ring.at[dst], is_.at[w, 4 + h], ir.at[w, 4 + h], at(dz=2 * h - 1))

    def y_sum(n):
        src = ring_rows(n // 2, OWN, (n % 2) * ACC, ACC)
        return remote(ring.at[src], fin.at[n - 1], fs.at[n - 1], fr.at[n - 1], at(dy=STEP[n]))

    pack(0, OWN)

    m_copies = []
    for i, (src, dst) in enumerate(((wg, ng), (wu, nu), (wd, nd), (ms, nm), (fm, nf), (sm, nsd))):
        m_copies.append(remote(src, dst, ms_s.at[i], ms_r.at[i], at(dy=2)))
    for cp in m_copies:
        cp.start()

    for cp in y_rows[1:]:
        cp.wait_recv()
    pack(1, OWN)
    for cp in w_copies[0::2]:
        cp.wait()
    for cp in w_copies[1::2]:
        cp.wait_recv()

    def tick(i, carry):
        w = jnp.where(i > 4, 1, 0)
        s = i - 4 * w
        first = 2 * s - 2

        @pl.when((i <= 8) & (s <= 3))
        def _():
            for h in range(2):
                dz = 1 - 2 * h

                @pl.when(i == 1)
                def _():
                    z_block(0, h, dz).wait_recv()
                    z_block(1, h, dz).wait_recv()

                @pl.when(i > 1)
                def _():
                    z_rows(w, first + h, first + h, dz).wait_recv()

                @pl.when(s < 3)
                def _():
                    z_rows(w, first + h, first + h + 2, dz).start()

                @pl.when(s == 3)
                def _():
                    z_half(w, h).start()

            @pl.when(i == 3)
            def _():
                z_rows(1, OWN, 0, 1).start()
                z_rows(1, OWN, 1, -1).start()

            @pl.when(i <= 3)
            def _():
                for h in range(2):
                    dz = 1 - 2 * h
                    z_meta(first + h, first + h, dz).wait_recv()

                    @pl.when(s < 3)
                    def _():
                        z_meta(first + h, first + h + 2, dz).start()

                @pl.when(s == 3)
                def _():
                    z_meta(4, 6, 1).start()

        @pl.when((i <= 8) & (s == 4))
        def _():
            z_half(w, 0).wait_recv()
            z_half(w, 1).wait_recv()

            @pl.when(i == 4)
            def _():
                z_meta(4, 6, 1).wait_recv()

        @pl.when(i <= 8)
        def _():
            @pl.loop(0, jnp.where(s == 4, 1, 2))
            def _(d):
                pack(w, first + d)

        @pl.when(i >= 9)
        def _():
            send_back_step(i - 9)

        @pl.when(i >= 3)
        def _():
            we = jnp.where(i > 6, 1, 0)
            expert(we, 2 * (i - 2 - 4 * we) - 2)

        return carry

    def wave_and_distance(r):
        w = jnp.where(r < 4, r // 2, lax.rem(r, 2))
        return w, jnp.where(r < 4, 4 - lax.rem(r, 2), 4 - r // 2)

    def send_back_step(r):
        w, s = wave_and_distance(r)

        @pl.when((r < 8) & (s == 4))
        def _():
            send_back(w, 6)

        @pl.when((r < 8) & (s < 4))
        def _():
            send_back(w, 2 * s - 1)
            send_back(w, 2 * s - 2)

        @pl.when(r >= 8)
        def _():
            send_back(r - 8, OWN)

    def return_step(r, carry):
        w, s = wave_and_distance(r)
        send_back_step(r + 2)

        @pl.when(s == 4)
        def _():
            combine(w, 6, (6,))
            r_half(w, 0).start()
            r_half(w, 1).start()

        @pl.when(s < 4)
        def _():
            @pl.loop(0, 2)
            def _(h):
                p = 2 * s - 1 - h
                dz = 1 - 2 * h

                @pl.when(s == 3)
                def _():
                    r_half(w, 1 - h).wait_recv()

                @pl.when(s < 3)
                def _():
                    r_rows(w, p, p, dz).wait_recv()

                combine(w, p, (p,))
                r_rows(w, p, jnp.where(p >= 2, p - 2, OWN + p), dz).start()

        return carry

    lax.fori_loop(1, 11, tick, 0)
    lax.fori_loop(0, 8, return_step, 0)

    @pl.loop(0, 2)
    def _(w):
        r_rows(w, 0, OWN, -1).wait_recv()
        r_rows(w, 1, OWN + 1, 1).wait_recv()
        combine(w, OWN, (OWN, OWN + 1))

        @pl.when(w == 0)
        def _():
            y_sum(1).start()

    y_sum(2).start()
    y_sum(3).start()

    for cp in m_copies:
        cp.wait()
    for cp in w_copies[1::2]:
        cp.wait_send()
    for cp in y_meta + y_rows:
        cp.wait_send()
    for p in range(7):
        z_meta(OWN, p, 1).wait_send()
    for p in range(2):
        z_rows(1, OWN, p, 1).wait_send()
        for b in range(2):
            z_block(b, p, 1).wait_send()

    @pl.loop(0, 2)
    def _(w):
        for p in range(2, 6):
            z_rows(w, OWN, p, 1).wait_send()
        for h in range(2):
            z_half(w, h).wait_send()
            r_half(w, h).wait_send()
        for slot in (0, 1, 2, 3, OWN, OWN + 1):
            r_rows(w, 0, slot, 1).wait_send()

        @pl.loop(0, 8)
        def _(p):
            for i in (1, 2, 3):
                x_send(w, p, i).wait_send()
                x_back(w, p, i).wait_send()

    for n in (1, 2, 3):
        y_sum(n).wait()
    dims = (((0,), (0,)), ((), ()))
    for n in range(NT):
        cols = slice(n * TILE, (n + 1) * TILE)
        v = ring[ring_rows(0, OWN, 0, ACC), cols].astype(F32)
        for i in range(3):
            v = v + fin[i, :, cols].astype(F32)
        out[:, cols] = lax.dot_general(pick[...], v.astype(BF), dims, preferred_element_type=F32).astype(BF)


def pieces(shape):
    lead, rows = (0,) * (len(shape) - 2), shape[-2]
    parts = 4 if rows % 64 == 0 else 1
    return [lead + (slice(i * rows // parts, (i + 1) * rows // parts),) for i in range(parts)]


def select(count, partner, *refs):
    arrived, held, whole = refs[:count], refs[count : 2 * count], refs[2 * count]
    outs = refs[2 * count + 1 : 3 * count + 2]
    stage, (loads, stores) = refs[3 * count + 2 : -2], refs[-2:]
    me = lax.axis_index("expert")
    moving = partner[me] != me
    work = [(a, i) for a in range(count + 1) for i in pieces(outs[a].shape)]

    def load(sources):
        for n, (a, i) in enumerate(work):
            if a < count:
                pltpu.make_async_copy(sources[a].at[i], stage[a].at[i], loads.at[n]).start()

    pl.when(moving)(lambda: load(arrived))
    pl.when(jnp.logical_not(moving))(lambda: load(held))
    for n, (a, i) in enumerate(work):
        if a == count:
            pltpu.make_async_copy(whole.at[i], stage[a].at[i], loads.at[n]).start()
    for n, (a, i) in enumerate(work):
        pltpu.make_async_copy(outs[a].at[i], stage[a].at[i], loads.at[n]).wait()
        pltpu.make_async_copy(stage[a].at[i], outs[a].at[i], stores.at[n]).start()
    for n, (a, i) in enumerate(work):
        pltpu.make_async_copy(stage[a].at[i], outs[a].at[i], stores.at[n]).wait()


def on_device(tokens, accepted, routes, gates, partner, w_gate, w_up, w_down, master_rows, first_moment, second_moment):
    held = (w_gate, w_up, w_down, master_rows, first_moment, second_moment)
    vmem = pl.BlockSpec(memory_space=pltpu.VMEM)
    anywhere = pl.BlockSpec(memory_space=pl.ANY)
    dma = pltpu.SemaphoreType.DMA
    combined, *arrived = pl.pallas_call(
        kernel,
        out_shape=[jax.ShapeDtypeStruct(tokens.shape, BF)]
        + [jax.ShapeDtypeStruct(a.shape, a.dtype) for a in held],
        in_specs=[vmem] * 4 + [anywhere] * 6,
        out_specs=[vmem] + [anywhere] * 6,
        scratch_shapes=[
            pltpu.VMEM((D, HID), BF),
            pltpu.VMEM((D, HID), BF),
            pltpu.VMEM((HID, D), BF),
            pltpu.VMEM((16 * UNIT, D), BF),
            pltpu.VMEM((16 * UNIT, D), BF),
            pltpu.VMEM((16 * UNIT, D), BF),
            pltpu.VMEM((16 * UNIT, D), BF),
            pltpu.VMEM((18 * UNIT, D), BF),
            pltpu.VMEM((3, ACC, D), BF),
            pltpu.VMEM((4, 16, TOK), F32),
            pltpu.VMEM((3, 16, TOK), F32),
            pltpu.VMEM((8, 16, TOK), F32),
            pltpu.VMEM((ACC, TOK), BF),
            pltpu.VMEM((16, UNIT, TOK), BF),
            pltpu.VMEM((16, UNIT, TOK), BF),
            pltpu.VMEM((2 * UNIT, HID), BF),
            dma((3,)), dma((3,)), dma((3,)), dma((3,)),
            dma((2, 10)), dma((2, 10)), dma((7,)), dma((7,)),
            dma((16, 3)), dma((16, 3)), dma((16, 3)), dma((16, 3)),
            dma((2, 9)), dma((2, 9)),
            dma((3,)), dma((3,)),
            dma((3,)), dma((3,)), dma((3,)),
            dma((6,)), dma((6,)),
        ],
        compiler_params=pltpu.CompilerParams(
            collective_id=0, has_side_effects=True, vmem_limit_bytes=60 << 20
        ),
        cost_estimate=pl.CostEstimate(flops=12 * 1024 * D * HID, bytes_accessed=24 << 20, transcendentals=1024 * HID),
        name="experts",
    )(tokens, accepted.reshape(1, -1), routes.T, gates.T, *held)
    count = len(held)
    hbm = pl.BlockSpec(memory_space=pltpu.HBM)
    outs = [jax.ShapeDtypeStruct(a.shape, a.dtype) for a in (*held, combined)]
    work = sum(len(pieces(a.shape)) for a in outs)
    *moved, combined = pl.pallas_call(
        functools.partial(select, count),
        out_shape=outs,
        in_specs=[pl.BlockSpec(memory_space=pltpu.SMEM)] + [hbm] * (2 * count + 1),
        out_specs=[hbm] * (count + 1),
        scratch_shapes=[pltpu.VMEM(a.shape, a.dtype) for a in outs] + [dma((work,)), dma((work,))],
        compiler_params=pltpu.CompilerParams(vmem_limit_bytes=60 << 20),
        name="select",
    )(partner, *arrived, *held, combined)
    return (combined, *moved)


def solution(mesh):
    both = P(("expert", "zero"), None)
    cols = P("expert", None, "zero")
    rows = P("expert", "zero", None)
    return jax.shard_map(
        on_device,
        mesh=mesh,
        in_specs=(both, P(("expert", "zero")), both, both, P(), cols, cols, rows, rows, rows, rows),
        out_specs=(both, cols, cols, rows, rows, rows, rows),
        check_vma=False,
    )
```

```python
import functools

import jax
import jax.numpy as jnp
from jax import lax
from jax.experimental import pallas as pl
from jax.experimental.pallas import tpu as pltpu
from jax.sharding import PartitionSpec as P

MESH = pl.DeviceIdType.MESH
BF = jnp.bfloat16
F32 = jnp.float32

D = 3584
ACC = 32
CAP = 8
TOK = 128
NX, NY, NZ = 4, 4, 8
UNIT = 2 * ACC
GROUP = UNIT // 4
OWN = 7
STEP = (0, 2, 1, 3)
HID = 512
TILE = 1792
NT = D // TILE


def unit_rows(w, p, first=0, count=UNIT):
    if isinstance(w, int) and isinstance(p, int):
        return pl.ds((w * 8 + p) * UNIT + first, count)
    return pl.ds(pl.multiple_of((w * 8 + p) * UNIT + first, 16), count)


def ring_rows(w, slot, first=0, count=UNIT):
    if isinstance(w, int) and isinstance(slot, int):
        return pl.ds((w * 9 + slot) * UNIT + first, count)
    return pl.ds(pl.multiple_of((w * 9 + slot) * UNIT + first, 16), count)


def tile(t):
    return pl.ds(t * TILE, TILE)


def kernel(
    tok_hbm, acc, rt, gt, wg, wu, wd, ms, fm, sm,
    out, ng, nu, nd, nm, nf, nsd,
    tok, tok_sem, w_g, w_u, w_d, gat, pck, rcv, ret, ring, fin, meta_y, meta_in, meta, pick, wt_hi, wt_lo, hid,
    ys, yr, yms, ymr, zs, zr, zms, zmr, xs, xr, bs, br, is_, ir, fs, fr, ls, ws, wr, ms_s, ms_r,
    yts, ytr, oxs, oxr, obs, obr, rts, rtr,
):
    e = lax.axis_index("expert")
    q = lax.axis_index("zero")
    y, zh, x = e // 16, lax.rem(e // 4, 4), lax.rem(e, 4)
    zl, c = q // 2, lax.rem(q, 2)
    z = zh * 2 + zl

    def at(dy=0, dz=0, dx=0, dc=0):
        yy = lax.rem(y + dy + NY, NY)
        zz = lax.rem(z + dz + NZ, NZ)
        xx = lax.rem(x + dx + NX, NX)
        cc = lax.rem(c + dc, 2)
        return (yy * 16 + (zz // 2) * 4 + xx, lax.rem(zz, 2) * 2 + cc)

    def remote(src, dst, ssem, rsem, dev):
        return pltpu.make_async_remote_copy(src, dst, ssem, rsem, device_id=dev, device_id_type=MESH)

    barrier = pltpu.get_barrier_semaphore()
    peers = [at(dy=i) for i in (1, 2, 3)] + [at(dx=i) for i in (1, 2, 3)]
    peers += [at(dz=1), at(dz=-1), at(dc=1)]
    for dev in peers:
        pl.semaphore_signal(barrier, inc=1, device_id=dev, device_id_type=MESH)

    tok_copy = pltpu.make_async_copy(tok_hbm, tok, tok_sem)
    tok_copy.start()

    r128 = lax.broadcasted_iota(jnp.int32, (TOK, TOK), 0)
    c128 = lax.broadcasted_iota(jnp.int32, (TOK, TOK), 1)
    acc_row = acc[...].astype(F32)
    spread = jnp.broadcast_to(acc_row, (TOK, TOK))
    acc_col = jnp.sum(jnp.where(r128 == c128, spread, 0.0), axis=1, keepdims=True)
    rank_col = jnp.sum(jnp.where(c128 < r128, spread, 0.0), axis=1, keepdims=True)
    rank_row = jnp.sum(
        jnp.where(r128 < c128, jnp.broadcast_to(acc_col, (TOK, TOK)), 0.0), axis=0, keepdims=True
    )
    i32r = lax.broadcasted_iota(jnp.int32, (ACC, TOK), 0).astype(F32)
    sel = jnp.where((rank_row == i32r) & (acc_row > 0.5), 1.0, 0.0).astype(BF)
    pick[...] = sel
    own_block = unit_rows(0, OWN, 0, ACC)
    tok_copy.wait()
    for n in range(NT):
        cols = slice(n * TILE, (n + 1) * TILE)
        gat[own_block, cols] = jnp.dot(sel, tok[:, cols], preferred_element_type=F32).astype(BF)
    pl.semaphore_wait(barrier, len(peers))

    y_meta, y_rows = [], []
    for n in (1, 2, 3):
        dev = at(dy=-STEP[n])
        dst = unit_rows(n // 2, OWN, (n % 2) * ACC, ACC)
        y_meta.append(remote(meta_y.at[n], meta_in.at[n - 1], yms.at[n - 1], ymr.at[n - 1], dev))
        if n > 1:
            y_rows.append(remote(gat.at[own_block], gat.at[dst], ys.at[n - 2], yr.at[n - 2], dev))
    first_block = unit_rows(0, OWN, ACC, ACC)

    def y_first(t):
        src, dst = gat.at[own_block, tile(t)], gat.at[first_block, tile(t)]
        return remote(src, dst, yts.at[t], ytr.at[t], at(dy=-STEP[1]))

    for t in range(NT):
        y_first(t).start()

    def z_block(b, to, dz):
        src, dst = unit_rows(0, OWN, b * ACC, ACC), unit_rows(0, to, b * ACC, ACC)
        n = to if b == 0 else 8 + to
        return remote(gat.at[src], gat.at[dst], zs.at[0, n], zr.at[0, n], at(dz=dz))

    z_block(0, 0, 1).start()
    z_block(0, 1, -1).start()

    wide = lax.broadcasted_iota(jnp.int32, (TOK, NY * TOK), 1)
    offset = (wide // TOK) * (TOK + ACC)
    here = (rank_col + offset.astype(F32) == wide.astype(F32)) & (acc_col > 0.5)
    sel2 = jnp.where(here, 1.0, 0.0).astype(BF)
    g_all = gt[...]
    g_hi = g_all.astype(BF).astype(F32)
    g_mid = (g_all - g_hi).astype(BF).astype(F32)
    g_lo = g_all - g_hi - g_mid
    stack = jnp.concatenate([rt[...].astype(F32), g_hi, g_mid, g_lo], axis=0).astype(BF)
    placed = jnp.dot(stack, sel2, preferred_element_type=F32)
    for j in range(NY):
        part = placed[:, j * TOK : (j + 1) * TOK]
        meta_y[j, 0:8, :] = part[0:8]
        meta_y[j, 8:16, :] = part[8:16] + part[16:24] + part[24:32]
    for cp in y_meta:
        cp.start()

    cols_c = pl.ds(pl.multiple_of(c * 256, 256), 256)
    w_pairs = [
        (wg.at[0], w_g.at[:, cols_c]),
        (wu.at[0], w_u.at[:, cols_c]),
        (wd.at[0], w_d.at[cols_c]),
    ]
    w_copies = []
    for i, (src, dst) in enumerate(w_pairs):
        w_copies.append(pltpu.make_async_copy(src, dst, ls.at[i]))
        w_copies.append(remote(src, dst, ws.at[i], wr.at[i], at(dc=1)))
    for cp in w_copies:
        cp.start()

    def z_rows(w, p, to, dz):
        return remote(gat.at[unit_rows(w, p)], gat.at[unit_rows(w, to)], zs.at[w, to], zr.at[w, to], at(dz=dz))

    def z_half(w, h):
        src, dst = unit_rows(w, 4 + h, h * ACC, ACC), unit_rows(w, 6, h * ACC, ACC)
        return remote(gat.at[src], gat.at[dst], zs.at[w, 6 + h], zr.at[w, 6 + h], at(dz=1 - 2 * h))

    def z_meta(p, to, dz):
        return remote(meta.at[p], meta.at[to], zms.at[to], zmr.at[to], at(dz=dz))

    for cp in y_meta:
        cp.wait_recv()
    meta[OWN] = meta_y[0] + meta_in[0] + meta_in[1] + meta_in[2]
    z_meta(OWN, 0, 1).start()
    z_meta(OWN, 1, -1).start()

    base = (e - x).astype(F32)

    def x_send(w, p, i):
        r = unit_rows(w, p, i * GROUP, GROUP)
        return remote(pck.at[r], rcv.at[r], xs.at[w * 8 + p, i - 1], xr.at[w * 8 + p, i - 1], at(dx=i))

    def x_back(w, p, i):
        r = unit_rows(w, p, i * GROUP, GROUP)
        return remote(rcv.at[r], ret.at[r], bs.at[w * 8 + p, i - 1], br.at[w * 8 + p, i - 1], at(dx=-i))

    def own_send(i, t):
        r = unit_rows(0, OWN, i * GROUP, GROUP)
        return remote(pck.at[r, tile(t)], rcv.at[r, tile(t)], oxs.at[i - 1, t], oxr.at[i - 1, t], at(dx=i))

    def own_back(w, i, t):
        r = unit_rows(w, OWN, i * GROUP, GROUP)
        return remote(rcv.at[r, tile(t)], ret.at[r, tile(t)], obs.at[w, i - 1, t], obr.at[w, i - 1, t], at(dx=-i))

    def plan(w, p):
        m = meta[p]
        m = jnp.where(w == 0, m, pltpu.roll(m, UNIT, 1))
        routes, gates = m[0:8], m[8:16]
        i16 = lax.broadcasted_iota(jnp.int32, (16, TOK), 0)
        want = base + lax.rem(x + i16, NX).astype(F32)
        hit = jnp.zeros((16, TOK), F32)
        weight = jnp.zeros((16, TOK), F32)
        for j in range(8):
            same = routes[j : j + 1] == want
            hit = hit + jnp.where(same, 1.0, 0.0)
            weight = weight + jnp.where(same, gates[j : j + 1], 0.0)
        earlier = jnp.where((r128 // ACC == c128 // ACC) & (r128 < c128), 1.0, 0.0).astype(BF)
        rank = jnp.dot(hit.astype(BF), earlier, preferred_element_type=F32)
        lane_group = (lax.broadcasted_iota(jnp.int32, (16, TOK), 1) // ACC).astype(F32)
        code = jnp.where(hit > 0.5, lane_group * CAP + rank, -1.0)
        ones, his, los = [], [], []
        for i in range(4):
            one = jnp.where(code[i : i + 1] == i32r[0:GROUP], 1.0, 0.0)
            scaled = one * weight[i : i + 1]
            hi = scaled.astype(BF).astype(F32)
            ones.append(one)
            his.append(hi)
            los.append(scaled - hi)
        place = jnp.concatenate(ones, axis=0).astype(BF)[:, 0:UNIT]
        wt_hi[w * 8 + p] = jnp.concatenate(his, axis=0).astype(BF)
        wt_lo[w * 8 + p] = jnp.concatenate(los, axis=0).astype(BF)
        return place

    def pack_tile(w, p, place, cols):
        v = jnp.dot(place, gat[unit_rows(w, p), cols], preferred_element_type=F32).astype(BF)
        rcv[unit_rows(w, p, 0, GROUP), cols] = v[:GROUP]
        pck[unit_rows(w, p, GROUP, UNIT - GROUP), cols] = v[GROUP:]

    def pack(w, p):
        place = plan(w, p)

        @pl.loop(0, NT)
        def _(n):
            pack_tile(w, p, place, pl.ds(pl.multiple_of(n * TILE, TILE), TILE))

        for i in (1, 2, 3):
            x_send(w, p, i).start()

    def expert(w, p):
        for i in (1, 2, 3):
            x_send(w, p, i).wait_recv()
        whole = (w == 1) | (p + 1 != OWN)

        @pl.when(whole)
        def _():
            for i in (1, 2, 3):
                x_send(w, p + 1, i).wait_recv()

        @pl.when(jnp.logical_not(whole))
        def _():
            for i in (1, 2, 3):
                for t in range(NT):
                    own_send(i, t).wait_recv()

        rows = rcv[unit_rows(w, p, 0, 2 * UNIT), :]
        gate = jnp.dot(rows, w_g[...], preferred_element_type=F32)
        up = jnp.dot(rows, w_u[...], preferred_element_type=F32)
        hid[...] = (gate / (1.0 + jnp.exp(-gate)) * up).astype(BF)

        @pl.loop(0, NT)
        def _(t):
            cols = pl.ds(pl.multiple_of(t * TILE, TILE), TILE)
            v = jnp.dot(hid[...], w_d[:, cols], preferred_element_type=F32).astype(BF)
            rcv[unit_rows(w, p, 0, 2 * UNIT), cols] = v
            for d in range(2):
                ret[unit_rows(w, p + d, 0, GROUP), cols] = v[d * UNIT : d * UNIT + GROUP]

    def send_back(w, p):
        for i in (1, 2, 3):
            x_back(w, p, i).start()

    def add_tile(w, p, slots, cols):
        hi, lo = wt_hi[w * 8 + p][:, 0:UNIT], wt_lo[w * 8 + p][:, 0:UNIT]
        part = ret[unit_rows(w, p), cols]
        dims = (((0,), (0,)), ((), ()))
        v = lax.dot_general(hi, part, dims, preferred_element_type=F32)
        v = v + lax.dot_general(lo, part, dims, preferred_element_type=F32)
        for s in slots:
            v = v + ring[ring_rows(w, s), cols].astype(F32)
        ring[ring_rows(w, slots[0]), cols] = v.astype(BF)

    def combine(w, p, slots):
        for i in (1, 2, 3):
            x_back(w, p, i).wait_recv()

        @pl.loop(0, NT)
        def _(n):
            add_tile(w, p, slots, pl.ds(pl.multiple_of(n * TILE, TILE), TILE))

    def r_rows(w, p, to, dz):
        return remote(ring.at[ring_rows(w, p)], ring.at[ring_rows(w, to)], is_.at[w, to], ir.at[w, to], at(dz=dz))

    def r_tile(w, p, t, dz):
        src, dst = ring.at[ring_rows(w, p), tile(t)], ring.at[ring_rows(w, OWN + p), tile(t)]
        return remote(src, dst, rts.at[w, p, t], rtr.at[w, p, t], at(dz=dz))

    def r_half(w, h):
        src, dst = ring_rows(w, 6, h * ACC, ACC), ring_rows(w, 4 + h, h * ACC, ACC)
        return remote(ring.at[src], ring.at[dst], is_.at[w, 4 + h], ir.at[w, 4 + h], at(dz=2 * h - 1))

    def y_sum(n, t):
        src, cols = ring_rows(n // 2, OWN, (n % 2) * ACC, ACC), pl.ds(t * TILE, TILE)
        return remote(
            ring.at[src, cols], fin.at[n - 1, :, cols], fs.at[n - 1, t], fr.at[n - 1, t], at(dy=STEP[n])
        )

    place = plan(0, OWN)
    for t in range(NT):
        y_first(t).wait_recv()
        if t == NT - 1:
            z_block(1, 0, 1).start()
            z_block(1, 1, -1).start()
            for cp in y_rows:
                cp.start()
        pack_tile(0, OWN, place, tile(t))
        for i in (1, 2, 3):
            own_send(i, t).start()

    m_copies = []
    for i, (src, dst) in enumerate(((wg, ng), (wu, nu), (wd, nd), (ms, nm), (fm, nf), (sm, nsd))):
        m_copies.append(remote(src, dst, ms_s.at[i], ms_r.at[i], at(dy=2)))
    for cp in m_copies:
        cp.start()

    for cp in y_rows:
        cp.wait_recv()
    pack(1, OWN)
    for w in range(2):
        ring[ring_rows(w, 6), :] = jnp.zeros((UNIT, D), BF)
        ring[ring_rows(w, 4, ACC, ACC), :] = jnp.zeros((ACC, D), BF)
        ring[ring_rows(w, 5, 0, ACC), :] = jnp.zeros((ACC, D), BF)

    for cp in w_copies[0::2]:
        cp.wait()
    for cp in w_copies[1::2]:
        cp.wait_recv()

    def tick(i, carry):
        w = jnp.where(i > 4, 1, 0)
        s = i - 4 * w
        first = 2 * s - 2

        @pl.when((i <= 8) & (s <= 3))
        def _():
            for h in range(2):
                dz = 1 - 2 * h

                @pl.when(i == 1)
                def _():
                    z_block(0, h, dz).wait_recv()
                    z_block(1, h, dz).wait_recv()

                @pl.when(i > 1)
                def _():
                    z_rows(w, first + h, first + h, dz).wait_recv()

                @pl.when(s < 3)
                def _():
                    z_rows(w, first + h, first + h + 2, dz).start()

                @pl.when(s == 3)
                def _():
                    z_half(w, h).start()

            @pl.when(i == 3)
            def _():
                z_rows(1, OWN, 0, 1).start()
                z_rows(1, OWN, 1, -1).start()

            @pl.when(i <= 3)
            def _():
                for h in range(2):
                    dz = 1 - 2 * h
                    z_meta(first + h, first + h, dz).wait_recv()

                    @pl.when(s < 3)
                    def _():
                        z_meta(first + h, first + h + 2, dz).start()

                @pl.when(s == 3)
                def _():
                    z_meta(4, 6, 1).start()

        @pl.when((i <= 8) & (s == 4))
        def _():
            z_half(w, 0).wait_recv()
            z_half(w, 1).wait_recv()

            @pl.when(i == 4)
            def _():
                z_meta(4, 6, 1).wait_recv()

        @pl.when(i <= 8)
        def _():
            @pl.loop(0, jnp.where(s == 4, 1, 2))
            def _(d):
                pack(w, first + d)

        @pl.when((i == 8) | (i == 9))
        def _():
            send_back_step(i - 8)

        @pl.when(i >= 3)
        def _():
            we = jnp.where(i > 6, 1, 0)
            expert(we, 2 * (i - 2 - 4 * we) - 2)

        return carry

    def wave_and_distance(r):
        w = jnp.where(r < 4, r // 2, lax.rem(r, 2))
        return w, jnp.where(r < 4, 4 - lax.rem(r, 2), 4 - r // 2)

    def send_back_step(r):
        w, s = wave_and_distance(r)

        @pl.when((r < 8) & (s == 4))
        def _():
            send_back(w, 6)

        @pl.when((r < 8) & (s < 4))
        def _():
            send_back(w, 2 * s - 1)
            send_back(w, 2 * s - 2)

        @pl.when(r >= 8)
        def _():
            for t in range(NT):
                for i in (1, 2, 3):
                    own_back(r - 8, i, t).start()

    def return_step(r, carry):
        w, s = wave_and_distance(r)
        send_back_step(r + 2)

        @pl.when(s == 4)
        def _():
            combine(w, 6, (6,))
            r_half(w, 0).start()
            r_half(w, 1).start()

        @pl.when(s < 4)
        def _():
            @pl.loop(0, 2)
            def _(h):
                p = 2 * s - 1 - h
                dz = 1 - 2 * h

                @pl.when(s == 3)
                def _():
                    r_half(w, 1 - h).wait_recv()

                @pl.when(s < 3)
                def _():
                    r_rows(w, p, p, dz).wait_recv()

                @pl.when(s > 1)
                def _():
                    combine(w, p, (p,))
                    r_rows(w, p, p - 2, dz).start()

                @pl.when(s == 1)
                def _():
                    for i in (1, 2, 3):
                        x_back(w, p, i).wait_recv()
                    for t in range(NT):
                        add_tile(w, p, (p,), tile(t))
                        r_tile(w, p, t, dz).start()

        return carry

    lax.fori_loop(1, 11, tick, 0)
    lax.fori_loop(0, 8, return_step, 0)

    for w in range(2):
        for t in range(NT):
            r_tile(w, 0, t, -1).wait_recv()
            r_tile(w, 1, t, 1).wait_recv()
            for i in (1, 2, 3):
                own_back(w, i, t).wait_recv()
            add_tile(w, OWN, (OWN, OWN + 1), tile(t))
            for n in ((1,), (2, 3))[w]:
                y_sum(n, t).start()

    for cp in m_copies:
        cp.wait()
    for cp in w_copies[1::2]:
        cp.wait_send()
    for cp in y_meta + y_rows:
        cp.wait_send()
    for p in range(7):
        z_meta(OWN, p, 1).wait_send()
    for p in range(2):
        z_rows(1, OWN, p, 1).wait_send()
        for b in range(2):
            z_block(b, p, 1).wait_send()

    @pl.loop(0, 2)
    def _(w):
        for p in range(2, 6):
            z_rows(w, OWN, p, 1).wait_send()
        for h in range(2):
            z_half(w, h).wait_send()
            r_half(w, h).wait_send()
        for slot in range(4):
            r_rows(w, 0, slot, 1).wait_send()
        for t in range(NT):
            for p in range(2):
                r_tile(w, p, t, 1).wait_send()
            for i in (1, 2, 3):
                own_back(w, i, t).wait_send()

        @pl.loop(0, OWN)
        def _(p):
            for i in (1, 2, 3):
                x_send(w, p, i).wait_send()
                x_back(w, p, i).wait_send()

    for i in (1, 2, 3):
        x_send(1, OWN, i).wait_send()
        for t in range(NT):
            own_send(i, t).wait_send()
    for t in range(NT):
        y_first(t).wait_send()

    dims = (((0,), (0,)), ((), ()))
    for t in range(NT):
        for n in (1, 2, 3):
            y_sum(n, t).wait()
        cols = slice(t * TILE, (t + 1) * TILE)
        v = ring[ring_rows(0, OWN, 0, ACC), cols].astype(F32)
        for i in range(3):
            v = v + fin[i, :, cols].astype(F32)
        out[:, cols] = lax.dot_general(pick[...], v.astype(BF), dims, preferred_element_type=F32).astype(BF)


def pieces(shape):
    lead, rows = (0,) * (len(shape) - 2), shape[-2]
    parts = 4 if rows % 64 == 0 else 1
    return [lead + (slice(i * rows // parts, (i + 1) * rows // parts),) for i in range(parts)]


def select(count, partner, *refs):
    arrived, held, whole = refs[:count], refs[count : 2 * count], refs[2 * count]
    outs = refs[2 * count + 1 : 3 * count + 2]
    stage, (loads, stores) = refs[3 * count + 2 : -2], refs[-2:]
    me = lax.axis_index("expert")
    moving = partner[me] != me
    work = [(a, i) for a in range(count + 1) for i in pieces(outs[a].shape)]

    def load(sources):
        for n, (a, i) in enumerate(work):
            if a < count:
                pltpu.make_async_copy(sources[a].at[i], stage[a].at[i], loads.at[n]).start()

    pl.when(moving)(lambda: load(arrived))
    pl.when(jnp.logical_not(moving))(lambda: load(held))
    for n, (a, i) in enumerate(work):
        if a == count:
            pltpu.make_async_copy(whole.at[i], stage[a].at[i], loads.at[n]).start()
    for n, (a, i) in enumerate(work):
        pltpu.make_async_copy(outs[a].at[i], stage[a].at[i], loads.at[n]).wait()
        pltpu.make_async_copy(stage[a].at[i], outs[a].at[i], stores.at[n]).start()
    for n, (a, i) in enumerate(work):
        pltpu.make_async_copy(stage[a].at[i], outs[a].at[i], stores.at[n]).wait()


def on_device(tokens, accepted, routes, gates, partner, w_gate, w_up, w_down, master_rows, first_moment, second_moment):
    held = (w_gate, w_up, w_down, master_rows, first_moment, second_moment)
    vmem = pl.BlockSpec(memory_space=pltpu.VMEM)
    anywhere = pl.BlockSpec(memory_space=pl.ANY)
    dma = pltpu.SemaphoreType.DMA
    combined, *arrived = pl.pallas_call(
        kernel,
        out_shape=[jax.ShapeDtypeStruct(tokens.shape, BF)]
        + [jax.ShapeDtypeStruct(a.shape, a.dtype) for a in held],
        in_specs=[anywhere] + [vmem] * 3 + [anywhere] * 6,
        out_specs=[vmem] + [anywhere] * 6,
        scratch_shapes=[
            pltpu.VMEM((TOK, D), BF),
            dma,
            pltpu.VMEM((D, HID), BF),
            pltpu.VMEM((D, HID), BF),
            pltpu.VMEM((HID, D), BF),
            pltpu.VMEM((16 * UNIT, D), BF),
            pltpu.VMEM((16 * UNIT, D), BF),
            pltpu.VMEM((16 * UNIT, D), BF),
            pltpu.VMEM((16 * UNIT, D), BF),
            pltpu.VMEM((18 * UNIT, D), BF),
            pltpu.VMEM((3, ACC, D), BF),
            pltpu.VMEM((4, 16, TOK), F32),
            pltpu.VMEM((3, 16, TOK), F32),
            pltpu.VMEM((8, 16, TOK), F32),
            pltpu.VMEM((ACC, TOK), BF),
            pltpu.VMEM((16, UNIT, TOK), BF),
            pltpu.VMEM((16, UNIT, TOK), BF),
            pltpu.VMEM((2 * UNIT, HID), BF),
            dma((2,)), dma((2,)), dma((3,)), dma((3,)),
            dma((2, 10)), dma((2, 10)), dma((7,)), dma((7,)),
            dma((16, 3)), dma((16, 3)), dma((16, 3)), dma((16, 3)),
            dma((2, 9)), dma((2, 9)),
            dma((3, NT)), dma((3, NT)),
            dma((3,)), dma((3,)), dma((3,)),
            dma((6,)), dma((6,)),
            dma((NT,)), dma((NT,)),
            dma((3, NT)), dma((3, NT)),
            dma((2, 3, NT)), dma((2, 3, NT)),
            dma((2, 2, NT)), dma((2, 2, NT)),
        ],
        compiler_params=pltpu.CompilerParams(
            collective_id=0, has_side_effects=True, vmem_limit_bytes=60 << 20
        ),
        cost_estimate=pl.CostEstimate(flops=12 * 1024 * D * HID, bytes_accessed=24 << 20, transcendentals=1024 * HID),
        name="experts",
    )(tokens, accepted.reshape(1, -1), routes.T, gates.T, *held)
    count = len(held)
    hbm = pl.BlockSpec(memory_space=pltpu.HBM)
    outs = [jax.ShapeDtypeStruct(a.shape, a.dtype) for a in (*held, combined)]
    work = sum(len(pieces(a.shape)) for a in outs)
    *moved, combined = pl.pallas_call(
        functools.partial(select, count),
        out_shape=outs,
        in_specs=[pl.BlockSpec(memory_space=pltpu.SMEM)] + [hbm] * (2 * count + 1),
        out_specs=[hbm] * (count + 1),
        scratch_shapes=[pltpu.VMEM(a.shape, a.dtype) for a in outs] + [dma((work,)), dma((work,))],
        compiler_params=pltpu.CompilerParams(vmem_limit_bytes=60 << 20),
        name="select",
    )(partner, *arrived, *held, combined)
    return (combined, *moved)


def solution(mesh):
    both = P(("expert", "zero"), None)
    cols = P("expert", None, "zero")
    rows = P("expert", "zero", None)
    return jax.shard_map(
        on_device,
        mesh=mesh,
        in_specs=(both, P(("expert", "zero")), both, both, P(), cols, cols, rows, rows, rows, rows),
        out_specs=(both, cols, cols, rows, rows, rows, rows),
        check_vma=False,
    )
```

```python
import functools

import jax
import jax.numpy as jnp
from jax import lax
from jax.experimental import pallas as pl
from jax.experimental.pallas import tpu as pltpu
from jax.sharding import PartitionSpec as P

MESH = pl.DeviceIdType.MESH
BF = jnp.bfloat16
F32 = jnp.float32

D = 3584
ACC = 32
CAP = 8
TOK = 128
NX, NY, NZ = 4, 4, 8
UNIT = 2 * ACC
GROUP = UNIT // 4
OWN = 7
STEP = (0, 2, 1, 3)
HID = 512
TILE = 1792
NT = D // TILE


def unit_rows(w, p, first=0, count=UNIT):
    if isinstance(w, int) and isinstance(p, int):
        return pl.ds((w * 8 + p) * UNIT + first, count)
    return pl.ds(pl.multiple_of((w * 8 + p) * UNIT + first, 16), count)


def ring_rows(w, slot, first=0, count=UNIT):
    if isinstance(w, int) and isinstance(slot, int):
        return pl.ds((w * 9 + slot) * UNIT + first, count)
    return pl.ds(pl.multiple_of((w * 9 + slot) * UNIT + first, 16), count)


def tile(t):
    return pl.ds(t * TILE, TILE)


def kernel(
    tok_hbm, acc, rt, gt, wg, wu, wd, ms, fm, sm,
    out, ng, nu, nd, nm, nf, nsd,
    tok, tok_sem, w_g, w_u, w_d, gat, pck, rcv, ret, ring, fin, meta_y, meta_in, meta, pick, wt_hi, wt_lo, hid,
    ys, yr, yms, ymr, zs, zr, zms, zmr, xs, xr, bs, br, is_, ir, fs, fr, ls, ws, wr, ms_s, ms_r,
    yts, ytr, oxs, oxr, obs, obr, rts, rtr,
):
    e = lax.axis_index("expert")
    q = lax.axis_index("zero")
    y, zh, x = e // 16, lax.rem(e // 4, 4), lax.rem(e, 4)
    zl, c = q // 2, lax.rem(q, 2)
    z = zh * 2 + zl

    def at(dy=0, dz=0, dx=0, dc=0):
        yy = lax.rem(y + dy + NY, NY)
        zz = lax.rem(z + dz + NZ, NZ)
        xx = lax.rem(x + dx + NX, NX)
        cc = lax.rem(c + dc, 2)
        return (yy * 16 + (zz // 2) * 4 + xx, lax.rem(zz, 2) * 2 + cc)

    def remote(src, dst, ssem, rsem, dev):
        return pltpu.make_async_remote_copy(src, dst, ssem, rsem, device_id=dev, device_id_type=MESH)

    barrier = pltpu.get_barrier_semaphore()
    peers = [at(dy=i) for i in (1, 2, 3)] + [at(dx=i) for i in (1, 2, 3)]
    peers += [at(dz=1), at(dz=-1), at(dc=1)]
    for dev in peers:
        pl.semaphore_signal(barrier, inc=1, device_id=dev, device_id_type=MESH)

    tok_copy = pltpu.make_async_copy(tok_hbm, tok, tok_sem)
    tok_copy.start()

    r128 = lax.broadcasted_iota(jnp.int32, (TOK, TOK), 0)
    c128 = lax.broadcasted_iota(jnp.int32, (TOK, TOK), 1)
    acc_row = acc[...].astype(F32)
    spread = jnp.broadcast_to(acc_row, (TOK, TOK))
    acc_col = jnp.sum(jnp.where(r128 == c128, spread, 0.0), axis=1, keepdims=True)
    rank_col = jnp.sum(jnp.where(c128 < r128, spread, 0.0), axis=1, keepdims=True)
    rank_row = jnp.sum(
        jnp.where(r128 < c128, jnp.broadcast_to(acc_col, (TOK, TOK)), 0.0), axis=0, keepdims=True
    )
    i32r = lax.broadcasted_iota(jnp.int32, (ACC, TOK), 0).astype(F32)
    sel = jnp.where((rank_row == i32r) & (acc_row > 0.5), 1.0, 0.0).astype(BF)
    pick[...] = sel
    own_block = unit_rows(0, OWN, 0, ACC)
    tok_copy.wait()
    for n in range(NT):
        cols = slice(n * TILE, (n + 1) * TILE)
        gat[own_block, cols] = jnp.dot(sel, tok[:, cols], preferred_element_type=F32).astype(BF)
    pl.semaphore_wait(barrier, len(peers))

    y_meta, y_rows = [], []
    for n in (1, 2, 3):
        dev = at(dy=-STEP[n])
        dst = unit_rows(n // 2, OWN, (n % 2) * ACC, ACC)
        y_meta.append(remote(meta_y.at[n], meta_in.at[n - 1], yms.at[n - 1], ymr.at[n - 1], dev))
        if n > 1:
            y_rows.append(remote(gat.at[own_block], gat.at[dst], ys.at[n - 2], yr.at[n - 2], dev))
    first_block = unit_rows(0, OWN, ACC, ACC)

    def y_first(t):
        src, dst = gat.at[own_block, tile(t)], gat.at[first_block, tile(t)]
        return remote(src, dst, yts.at[t], ytr.at[t], at(dy=-STEP[1]))

    for t in range(NT):
        y_first(t).start()

    def z_block(b, to, dz):
        src, dst = unit_rows(0, OWN, b * ACC, ACC), unit_rows(0, to, b * ACC, ACC)
        n = to if b == 0 else 8 + to
        return remote(gat.at[src], gat.at[dst], zs.at[0, n], zr.at[0, n], at(dz=dz))

    z_block(0, 0, 1).start()
    z_block(0, 1, -1).start()

    wide = lax.broadcasted_iota(jnp.int32, (TOK, NY * TOK), 1)
    offset = (wide // TOK) * (TOK + ACC)
    here = (rank_col + offset.astype(F32) == wide.astype(F32)) & (acc_col > 0.5)
    sel2 = jnp.where(here, 1.0, 0.0).astype(BF)
    g_all = gt[...]
    g_hi = g_all.astype(BF).astype(F32)
    g_mid = (g_all - g_hi).astype(BF).astype(F32)
    g_lo = g_all - g_hi - g_mid
    stack = jnp.concatenate([rt[...].astype(F32), g_hi, g_mid, g_lo], axis=0).astype(BF)
    placed = jnp.dot(stack, sel2, preferred_element_type=F32)
    for j in range(NY):
        part = placed[:, j * TOK : (j + 1) * TOK]
        meta_y[j, 0:8, :] = part[0:8]
        meta_y[j, 8:16, :] = part[8:16] + part[16:24] + part[24:32]
    for cp in y_meta:
        cp.start()

    cols_c = pl.ds(pl.multiple_of(c * 256, 256), 256)
    w_pairs = [
        (wg.at[0], w_g.at[:, cols_c]),
        (wu.at[0], w_u.at[:, cols_c]),
        (wd.at[0], w_d.at[cols_c]),
    ]
    w_copies = []
    for i, (src, dst) in enumerate(w_pairs):
        w_copies.append(pltpu.make_async_copy(src, dst, ls.at[i]))
        w_copies.append(remote(src, dst, ws.at[i], wr.at[i], at(dc=1)))
    for cp in w_copies:
        cp.start()

    def z_rows(w, p, to, dz):
        return remote(gat.at[unit_rows(w, p)], gat.at[unit_rows(w, to)], zs.at[w, to], zr.at[w, to], at(dz=dz))

    def z_half(w, h):
        src, dst = unit_rows(w, 4 + h, h * ACC, ACC), unit_rows(w, 6, h * ACC, ACC)
        return remote(gat.at[src], gat.at[dst], zs.at[w, 6 + h], zr.at[w, 6 + h], at(dz=1 - 2 * h))

    def z_meta(p, to, dz):
        return remote(meta.at[p], meta.at[to], zms.at[to], zmr.at[to], at(dz=dz))

    for cp in y_meta:
        cp.wait_recv()
    meta[OWN] = meta_y[0] + meta_in[0] + meta_in[1] + meta_in[2]
    z_meta(OWN, 0, 1).start()
    z_meta(OWN, 1, -1).start()

    base = (e - x).astype(F32)

    def x_send(w, p, i):
        r = unit_rows(w, p, i * GROUP, GROUP)
        return remote(pck.at[r], rcv.at[r], xs.at[w * 8 + p, i - 1], xr.at[w * 8 + p, i - 1], at(dx=i))

    def x_back(w, p, i):
        r = unit_rows(w, p, i * GROUP, GROUP)
        return remote(rcv.at[r], ret.at[r], bs.at[w * 8 + p, i - 1], br.at[w * 8 + p, i - 1], at(dx=-i))

    def own_send(i, t):
        r = unit_rows(0, OWN, i * GROUP, GROUP)
        return remote(pck.at[r, tile(t)], rcv.at[r, tile(t)], oxs.at[i - 1, t], oxr.at[i - 1, t], at(dx=i))

    def own_back(w, i, t):
        r = unit_rows(w, OWN, i * GROUP, GROUP)
        return remote(rcv.at[r, tile(t)], ret.at[r, tile(t)], obs.at[w, i - 1, t], obr.at[w, i - 1, t], at(dx=-i))

    def plan(w, p):
        m = meta[p]
        m = jnp.where(w == 0, m, pltpu.roll(m, UNIT, 1))
        routes, gates = m[0:8], m[8:16]
        i16 = lax.broadcasted_iota(jnp.int32, (16, TOK), 0)
        want = base + lax.rem(x + i16, NX).astype(F32)
        hit = jnp.zeros((16, TOK), F32)
        weight = jnp.zeros((16, TOK), F32)
        for j in range(8):
            same = routes[j : j + 1] == want
            hit = hit + jnp.where(same, 1.0, 0.0)
            weight = weight + jnp.where(same, gates[j : j + 1], 0.0)
        earlier = jnp.where((r128 // ACC == c128 // ACC) & (r128 < c128), 1.0, 0.0).astype(BF)
        rank = jnp.dot(hit.astype(BF), earlier, preferred_element_type=F32)
        lane_group = (lax.broadcasted_iota(jnp.int32, (16, TOK), 1) // ACC).astype(F32)
        code = jnp.where(hit > 0.5, lane_group * CAP + rank, -1.0)
        ones, his, los = [], [], []
        for i in range(4):
            one = jnp.where(code[i : i + 1] == i32r[0:GROUP], 1.0, 0.0)
            scaled = one * weight[i : i + 1]
            hi = scaled.astype(BF).astype(F32)
            ones.append(one)
            his.append(hi)
            los.append(scaled - hi)
        place = jnp.concatenate(ones, axis=0).astype(BF)[:, 0:UNIT]
        wt_hi[w * 8 + p] = jnp.concatenate(his, axis=0).astype(BF)
        wt_lo[w * 8 + p] = jnp.concatenate(los, axis=0).astype(BF)
        return place

    def pack_tile(w, p, place, cols):
        v = jnp.dot(place, gat[unit_rows(w, p), cols], preferred_element_type=F32).astype(BF)
        rcv[unit_rows(w, p, 0, GROUP), cols] = v[:GROUP]
        pck[unit_rows(w, p, GROUP, UNIT - GROUP), cols] = v[GROUP:]

    def pack(w, p):
        place = plan(w, p)

        @pl.loop(0, NT)
        def _(n):
            pack_tile(w, p, place, pl.ds(pl.multiple_of(n * TILE, TILE), TILE))

        for i in (1, 2, 3):
            x_send(w, p, i).start()

    def expert(w, p):
        for i in (1, 2, 3):
            x_send(w, p, i).wait_recv()
        whole = (w == 1) | (p + 1 != OWN)

        @pl.when(whole)
        def _():
            for i in (1, 2, 3):
                x_send(w, p + 1, i).wait_recv()

        @pl.when(jnp.logical_not(whole))
        def _():
            for i in (1, 2, 3):
                for t in range(NT):
                    own_send(i, t).wait_recv()

        rows = rcv[unit_rows(w, p, 0, 2 * UNIT), :]
        gate = jnp.dot(rows, w_g[...], preferred_element_type=F32)
        up = jnp.dot(rows, w_u[...], preferred_element_type=F32)
        hid[...] = (gate / (1.0 + jnp.exp(-gate)) * up).astype(BF)

        @pl.loop(0, NT)
        def _(t):
            cols = pl.ds(pl.multiple_of(t * TILE, TILE), TILE)
            v = jnp.dot(hid[...], w_d[:, cols], preferred_element_type=F32).astype(BF)
            rcv[unit_rows(w, p, 0, 2 * UNIT), cols] = v
            for d in range(2):
                ret[unit_rows(w, p + d, 0, GROUP), cols] = v[d * UNIT : d * UNIT + GROUP]

    def send_back(w, p):
        for i in (1, 2, 3):
            x_back(w, p, i).start()

    def add_tile(w, p, slots, cols):
        hi, lo = wt_hi[w * 8 + p][:, 0:UNIT], wt_lo[w * 8 + p][:, 0:UNIT]
        part = ret[unit_rows(w, p), cols]
        dims = (((0,), (0,)), ((), ()))
        v = lax.dot_general(hi, part, dims, preferred_element_type=F32)
        v = v + lax.dot_general(lo, part, dims, preferred_element_type=F32)
        for s in slots:
            v = v + ring[ring_rows(w, s), cols].astype(F32)
        ring[ring_rows(w, slots[0]), cols] = v.astype(BF)

    def combine(w, p, slots):
        for i in (1, 2, 3):
            x_back(w, p, i).wait_recv()

        @pl.loop(0, NT)
        def _(n):
            add_tile(w, p, slots, pl.ds(pl.multiple_of(n * TILE, TILE), TILE))

    def r_rows(w, p, to, dz):
        return remote(ring.at[ring_rows(w, p)], ring.at[ring_rows(w, to)], is_.at[w, to], ir.at[w, to], at(dz=dz))

    def r_tile(w, p, t, dz):
        src, dst = ring.at[ring_rows(w, p), tile(t)], ring.at[ring_rows(w, OWN + p), tile(t)]
        return remote(src, dst, rts.at[w, p, t], rtr.at[w, p, t], at(dz=dz))

    def r_half(w, h):
        src, dst = ring_rows(w, 6, h * ACC, ACC), ring_rows(w, 4 + h, h * ACC, ACC)
        return remote(ring.at[src], ring.at[dst], is_.at[w, 4 + h], ir.at[w, 4 + h], at(dz=2 * h - 1))

    def y_sum(n, t):
        src, cols = ring_rows(n // 2, OWN, (n % 2) * ACC, ACC), pl.ds(t * TILE, TILE)
        return remote(
            ring.at[src, cols], fin.at[n - 1, :, cols], fs.at[n - 1, t], fr.at[n - 1, t], at(dy=STEP[n])
        )

    place = plan(0, OWN)
    for t in range(NT):
        y_first(t).wait_recv()
        if t == NT - 1:
            z_block(1, 0, 1).start()
            z_block(1, 1, -1).start()
            for cp in y_rows:
                cp.start()
        pack_tile(0, OWN, place, tile(t))
        for i in (1, 2, 3):
            own_send(i, t).start()

    m_copies = []
    for i, (src, dst) in enumerate(((wg, ng), (wu, nu), (wd, nd), (ms, nm), (fm, nf), (sm, nsd))):
        m_copies.append(remote(src, dst, ms_s.at[i], ms_r.at[i], at(dy=2)))

    for cp in y_rows:
        cp.wait_recv()
    pack(1, OWN)
    for cp in m_copies:
        cp.start()
    for w in range(2):
        ring[ring_rows(w, 6), :] = jnp.zeros((UNIT, D), BF)
        ring[ring_rows(w, 4, ACC, ACC), :] = jnp.zeros((ACC, D), BF)
        ring[ring_rows(w, 5, 0, ACC), :] = jnp.zeros((ACC, D), BF)

    for cp in w_copies[0::2]:
        cp.wait()
    for cp in w_copies[1::2]:
        cp.wait_recv()

    def tick(i, carry):
        w = jnp.where(i > 4, 1, 0)
        s = i - 4 * w
        first = 2 * s - 2

        @pl.when((i <= 8) & (s <= 3))
        def _():
            for h in range(2):
                dz = 1 - 2 * h

                @pl.when(i == 1)
                def _():
                    z_block(0, h, dz).wait_recv()
                    z_block(1, h, dz).wait_recv()

                @pl.when(i > 1)
                def _():
                    z_rows(w, first + h, first + h, dz).wait_recv()

                @pl.when(s < 3)
                def _():
                    z_rows(w, first + h, first + h + 2, dz).start()

                @pl.when(s == 3)
                def _():
                    z_half(w, h).start()

            @pl.when(i == 3)
            def _():
                z_rows(1, OWN, 0, 1).start()
                z_rows(1, OWN, 1, -1).start()

            @pl.when(i <= 3)
            def _():
                for h in range(2):
                    dz = 1 - 2 * h
                    z_meta(first + h, first + h, dz).wait_recv()

                    @pl.when(s < 3)
                    def _():
                        z_meta(first + h, first + h + 2, dz).start()

                @pl.when(s == 3)
                def _():
                    z_meta(4, 6, 1).start()

        @pl.when((i <= 8) & (s == 4))
        def _():
            z_half(w, 0).wait_recv()
            z_half(w, 1).wait_recv()

            @pl.when(i == 4)
            def _():
                z_meta(4, 6, 1).wait_recv()

        @pl.when(i <= 8)
        def _():
            @pl.loop(0, jnp.where(s == 4, 1, 2))
            def _(d):
                pack(w, first + d)

        @pl.when((i == 8) | (i == 9))
        def _():
            send_back_step(i - 8)

        @pl.when(i >= 3)
        def _():
            we = jnp.where(i > 6, 1, 0)
            expert(we, 2 * (i - 2 - 4 * we) - 2)

        return carry

    def wave_and_distance(r):
        w = jnp.where(r < 4, r // 2, lax.rem(r, 2))
        return w, jnp.where(r < 4, 4 - lax.rem(r, 2), 4 - r // 2)

    def send_back_step(r):
        w, s = wave_and_distance(r)

        @pl.when((r < 8) & (s == 4))
        def _():
            send_back(w, 6)

        @pl.when((r < 8) & (s < 4))
        def _():
            send_back(w, 2 * s - 1)
            send_back(w, 2 * s - 2)

        @pl.when(r >= 8)
        def _():
            for t in range(NT):
                for i in (1, 2, 3):
                    own_back(r - 8, i, t).start()

    def return_step(r, carry):
        w, s = wave_and_distance(r)
        send_back_step(r + 2)

        @pl.when(s == 4)
        def _():
            combine(w, 6, (6,))
            r_half(w, 0).start()
            r_half(w, 1).start()

        @pl.when(s < 4)
        def _():
            @pl.loop(0, 2)
            def _(h):
                p = 2 * s - 1 - h
                dz = 1 - 2 * h

                @pl.when(s == 3)
                def _():
                    r_half(w, 1 - h).wait_recv()

                @pl.when(s < 3)
                def _():
                    r_rows(w, p, p, dz).wait_recv()

                @pl.when(s > 1)
                def _():
                    combine(w, p, (p,))
                    r_rows(w, p, p - 2, dz).start()

                @pl.when(s == 1)
                def _():
                    for i in (1, 2, 3):
                        x_back(w, p, i).wait_recv()
                    for t in range(NT):
                        add_tile(w, p, (p,), tile(t))
                        r_tile(w, p, t, dz).start()

        return carry

    lax.fori_loop(1, 11, tick, 0)
    lax.fori_loop(0, 8, return_step, 0)

    for w in range(2):
        for t in range(NT):
            r_tile(w, 0, t, -1).wait_recv()
            r_tile(w, 1, t, 1).wait_recv()
            for i in (1, 2, 3):
                own_back(w, i, t).wait_recv()
            add_tile(w, OWN, (OWN, OWN + 1), tile(t))
            for n in ((1,), (2, 3))[w]:
                y_sum(n, t).start()

    for cp in m_copies:
        cp.wait()
    for cp in w_copies[1::2]:
        cp.wait_send()
    for cp in y_meta + y_rows:
        cp.wait_send()
    for p in range(7):
        z_meta(OWN, p, 1).wait_send()
    for p in range(2):
        z_rows(1, OWN, p, 1).wait_send()
        for b in range(2):
            z_block(b, p, 1).wait_send()

    @pl.loop(0, 2)
    def _(w):
        for p in range(2, 6):
            z_rows(w, OWN, p, 1).wait_send()
        for h in range(2):
            z_half(w, h).wait_send()
            r_half(w, h).wait_send()
        for slot in range(4):
            r_rows(w, 0, slot, 1).wait_send()
        for t in range(NT):
            for p in range(2):
                r_tile(w, p, t, 1).wait_send()
            for i in (1, 2, 3):
                own_back(w, i, t).wait_send()

        @pl.loop(0, OWN)
        def _(p):
            for i in (1, 2, 3):
                x_send(w, p, i).wait_send()
                x_back(w, p, i).wait_send()

    for i in (1, 2, 3):
        x_send(1, OWN, i).wait_send()
        for t in range(NT):
            own_send(i, t).wait_send()
    for t in range(NT):
        y_first(t).wait_send()

    dims = (((0,), (0,)), ((), ()))
    for t in range(NT):
        for n in (1, 2, 3):
            y_sum(n, t).wait()
        cols = slice(t * TILE, (t + 1) * TILE)
        v = ring[ring_rows(0, OWN, 0, ACC), cols].astype(F32)
        for i in range(3):
            v = v + fin[i, :, cols].astype(F32)
        out[:, cols] = lax.dot_general(pick[...], v.astype(BF), dims, preferred_element_type=F32).astype(BF)


def pieces(shape):
    lead, rows = (0,) * (len(shape) - 2), shape[-2]
    parts = 4 if rows % 64 == 0 else 1
    return [lead + (slice(i * rows // parts, (i + 1) * rows // parts),) for i in range(parts)]


def select(count, partner, *refs):
    arrived, held, whole = refs[:count], refs[count : 2 * count], refs[2 * count]
    outs = refs[2 * count + 1 : 3 * count + 2]
    stage, (loads, stores) = refs[3 * count + 2 : -2], refs[-2:]
    me = lax.axis_index("expert")
    moving = partner[me] != me
    work = [(a, i) for a in range(count + 1) for i in pieces(outs[a].shape)]

    def load(sources):
        for n, (a, i) in enumerate(work):
            if a < count:
                pltpu.make_async_copy(sources[a].at[i], stage[a].at[i], loads.at[n]).start()

    pl.when(moving)(lambda: load(arrived))
    pl.when(jnp.logical_not(moving))(lambda: load(held))
    for n, (a, i) in enumerate(work):
        if a == count:
            pltpu.make_async_copy(whole.at[i], stage[a].at[i], loads.at[n]).start()
    for n, (a, i) in enumerate(work):
        pltpu.make_async_copy(outs[a].at[i], stage[a].at[i], loads.at[n]).wait()
        pltpu.make_async_copy(stage[a].at[i], outs[a].at[i], stores.at[n]).start()
    for n, (a, i) in enumerate(work):
        pltpu.make_async_copy(stage[a].at[i], outs[a].at[i], stores.at[n]).wait()


def on_device(tokens, accepted, routes, gates, partner, w_gate, w_up, w_down, master_rows, first_moment, second_moment):
    held = (w_gate, w_up, w_down, master_rows, first_moment, second_moment)
    vmem = pl.BlockSpec(memory_space=pltpu.VMEM)
    anywhere = pl.BlockSpec(memory_space=pl.ANY)
    dma = pltpu.SemaphoreType.DMA
    combined, *arrived = pl.pallas_call(
        kernel,
        out_shape=[jax.ShapeDtypeStruct(tokens.shape, BF)]
        + [jax.ShapeDtypeStruct(a.shape, a.dtype) for a in held],
        in_specs=[anywhere] + [vmem] * 3 + [anywhere] * 6,
        out_specs=[vmem] + [anywhere] * 6,
        scratch_shapes=[
            pltpu.VMEM((TOK, D), BF),
            dma,
            pltpu.VMEM((D, HID), BF),
            pltpu.VMEM((D, HID), BF),
            pltpu.VMEM((HID, D), BF),
            pltpu.VMEM((16 * UNIT, D), BF),
            pltpu.VMEM((16 * UNIT, D), BF),
            pltpu.VMEM((16 * UNIT, D), BF),
            pltpu.VMEM((16 * UNIT, D), BF),
            pltpu.VMEM((18 * UNIT, D), BF),
            pltpu.VMEM((3, ACC, D), BF),
            pltpu.VMEM((4, 16, TOK), F32),
            pltpu.VMEM((3, 16, TOK), F32),
            pltpu.VMEM((8, 16, TOK), F32),
            pltpu.VMEM((ACC, TOK), BF),
            pltpu.VMEM((16, UNIT, TOK), BF),
            pltpu.VMEM((16, UNIT, TOK), BF),
            pltpu.VMEM((2 * UNIT, HID), BF),
            dma((2,)), dma((2,)), dma((3,)), dma((3,)),
            dma((2, 10)), dma((2, 10)), dma((7,)), dma((7,)),
            dma((16, 3)), dma((16, 3)), dma((16, 3)), dma((16, 3)),
            dma((2, 9)), dma((2, 9)),
            dma((3, NT)), dma((3, NT)),
            dma((3,)), dma((3,)), dma((3,)),
            dma((6,)), dma((6,)),
            dma((NT,)), dma((NT,)),
            dma((3, NT)), dma((3, NT)),
            dma((2, 3, NT)), dma((2, 3, NT)),
            dma((2, 2, NT)), dma((2, 2, NT)),
        ],
        compiler_params=pltpu.CompilerParams(
            collective_id=0, has_side_effects=True, vmem_limit_bytes=60 << 20
        ),
        cost_estimate=pl.CostEstimate(flops=12 * 1024 * D * HID, bytes_accessed=24 << 20, transcendentals=1024 * HID),
        name="experts",
    )(tokens, accepted.reshape(1, -1), routes.T, gates.T, *held)
    count = len(held)
    hbm = pl.BlockSpec(memory_space=pltpu.HBM)
    outs = [jax.ShapeDtypeStruct(a.shape, a.dtype) for a in (*held, combined)]
    work = sum(len(pieces(a.shape)) for a in outs)
    *moved, combined = pl.pallas_call(
        functools.partial(select, count),
        out_shape=outs,
        in_specs=[pl.BlockSpec(memory_space=pltpu.SMEM)] + [hbm] * (2 * count + 1),
        out_specs=[hbm] * (count + 1),
        scratch_shapes=[pltpu.VMEM(a.shape, a.dtype) for a in outs] + [dma((work,)), dma((work,))],
        compiler_params=pltpu.CompilerParams(vmem_limit_bytes=60 << 20),
        name="select",
    )(partner, *arrived, *held, combined)
    return (combined, *moved)


def solution(mesh):
    both = P(("expert", "zero"), None)
    cols = P("expert", None, "zero")
    rows = P("expert", "zero", None)
    return jax.shard_map(
        on_device,
        mesh=mesh,
        in_specs=(both, P(("expert", "zero")), both, both, P(), cols, cols, rows, rows, rows, rows),
        out_specs=(both, cols, cols, rows, rows, rows, rows),
        check_vma=False,
    )
```
